32 devices in a mesh: gx: 8 (over z, y), gz: 4 (over x, core).
Axes of the slice: x: 2, y: 2, z: 4, core: 2. Of those that a mesh axis runs over, the one named last changes fastest.
Arguments:
- thermal_undercool: float32 [16, 384, 512], P(None, 'gx', 'gz'), may hold values from -1 to 1
- mixture_alloying: float32 [16, 384, 512], P(None, 'gx', 'gz'), may hold values from 0.5 to 1.5
- fluid_fraction: float32 [16, 384, 512], P(None, 'gx', 'gz'), may hold values from 0.05 to 0.95
- kozeny_factor: float32 [16, 384, 512], P(None, 'gx', 'gz'), may hold values from 0.5 to 2
- state_marker: int32 [16, 384, 512], P(None, 'gx', 'gz'), may hold values from 0 to 2
Outputs:
- pressure: float32 [16, 384, 512], P(None, 'gx', 'gz')
- solute_out: float32 [16, 384, 512], P(None, 'gx', 'gz')
The draws below stay inside these ranges and needn't reach their ends.
Inputs may be any that keep to these rules, and one draw needn't show every extreme that they name: `state_marker`: 0 marks a mushy cell, 1 a liquid one, 2 a solid one.
All inputs are finite; a program needn't handle non-finite values.
Results may differ from the reference program's by a relative error of at most 0.0003.
Values sent between devices are 32-bit elements; how exact they have to be, the bound alone decides.
A program may use at most 64 MiB of HBM per device.

```python
import math
import jax
import jax.numpy as jnp

SLAB_LAYER_COUNT = 16
STEPS = 4
SWEEPS = 3
MESH_WIDTH_COUNT = 384
MESH_DEPTH_COUNT = 512


def place_ends(array, key, smallest, high):
    index_at = [jax.random.randint(jax.random.fold_in(key, axis), (), 0, length) for axis, length in enumerate(array.shape)]
    widest = array.shape.index(max(array.shape))
    neighbour = index_at[:widest] + [(index_at[widest] + 1) % array.shape[widest]] + index_at[widest + 1:]
    return array.at[tuple(index_at)].set(smallest).at[tuple(neighbour)].set(high)


def block_levels(key, shape, split, smallest, high):
    gain, own = 1.0, jax.random.fold_in(key, 6)
    for dim, shards_of in split:
        draws = jnp.exp(jax.random.uniform(jax.random.fold_in(own, dim), (shards_of,), jnp.float32, smallest / len(split), high / len(split)))
        gain = gain * jnp.repeat(draws, shape[dim] // shards_of).reshape([-1 if axis == dim else 1 for axis in range(len(shape))])
    return gain


def setup_inputs(seed: int = 0) -> dict:
    key_list = jax.random.split(jax.random.key(seed), 6)
    thermal_undercool = jnp.clip(jax.random.uniform(key_list[0], (SLAB_LAYER_COUNT, MESH_WIDTH_COUNT, MESH_DEPTH_COUNT), jnp.float32, -1.0, 1.0) * block_levels(key_list[0], (SLAB_LAYER_COUNT, MESH_WIDTH_COUNT, MESH_DEPTH_COUNT), ((1, 8), (2, 4)), -0.4, 0.0), -1.0, 1.0)
    mixture_alloying = jnp.clip(0.5 + 1.0 * jax.random.uniform(key_list[1], (SLAB_LAYER_COUNT, MESH_WIDTH_COUNT, MESH_DEPTH_COUNT), jnp.float32) ** block_levels(key_list[1], (SLAB_LAYER_COUNT, MESH_WIDTH_COUNT, MESH_DEPTH_COUNT), ((1, 8), (2, 4)), -0.2, 0.2), 0.5, 1.5)
    fluid_fraction = jnp.clip(0.05 + 0.9 * jax.random.uniform(key_list[2], (SLAB_LAYER_COUNT, MESH_WIDTH_COUNT, MESH_DEPTH_COUNT), jnp.float32) ** block_levels(key_list[2], (SLAB_LAYER_COUNT, MESH_WIDTH_COUNT, MESH_DEPTH_COUNT), ((1, 8), (2, 4)), -0.2, 0.2), 0.05, 0.95)
    kozeny_factor = jnp.clip(jnp.exp(math.log(2.0) - 1.3862944 * jax.random.uniform(key_list[3], (SLAB_LAYER_COUNT, MESH_WIDTH_COUNT, MESH_DEPTH_COUNT), jnp.float32) ** block_levels(key_list[3], (SLAB_LAYER_COUNT, MESH_WIDTH_COUNT, MESH_DEPTH_COUNT), ((1, 8), (2, 4)), -0.2, 0.2)), 0.5, 2.0)
    state_marker = place_ends(jax.random.randint(key_list[4], (SLAB_LAYER_COUNT, MESH_WIDTH_COUNT, MESH_DEPTH_COUNT), 0, 3), jax.random.fold_in(key_list[4], 1), 0, 2).astype(jnp.int32)
    return dict(thermal_undercool=thermal_undercool, mixture_alloying=mixture_alloying, fluid_fraction=fluid_fraction, kozeny_factor=kozeny_factor, state_marker=state_marker)


solute_rate = 0.5


def zero_rim(field):
    return jnp.pad(field, ((0, 0), (1, 1), (1, 1)))


def neighbours_of(extended):
    center = extended[:, 1:-1, 1:-1]
    padded = jnp.pad(center, ((1, 1), (0, 0), (0, 0)))
    return center, [extended[:, 2:, 1:-1], extended[:, :-2, 1:-1], padded[2:], padded[:-2], extended[:, 1:-1, 2:], extended[:, 1:-1, :-2]]


def face_terms(perm_ext, density_ext, gravity):
    perm_mid, perm_near = neighbours_of(perm_ext)
    density_mid, density_near = neighbours_of(density_ext)
    conductance = [0.5 * (perm_mid + other) for other in perm_near]
    diagonal = conductance[0]
    for face_index in range(1, 6):
        diagonal = diagonal + conductance[face_index]
    lift_down = gravity * 0.5 * (density_mid + density_near[4])
    lift_up = -(gravity * 0.5 * (density_mid + density_near[5]))
    return conductance, diagonal, lift_down, lift_up


def jacobi_sweep(pressure_ext, coupling, forcing_amount):
    conductance, diagonal, lift_down, lift_up = coupling
    _, pressure_near = neighbours_of(pressure_ext)
    numerator = forcing_amount - conductance[4] * lift_down - conductance[5] * lift_up
    for face_index in range(6):
        numerator = numerator + conductance[face_index] * pressure_near[face_index]
    return numerator / diagonal


def solute_update(pressure_ext, conc_ext, coupling, molten_state):
    conductance, _, lift_down, lift_up = coupling
    pressure_mid, pressure_near = neighbours_of(pressure_ext)
    conc_mid, conc_near = neighbours_of(conc_ext)
    change = jnp.zeros_like(conc_mid)
    for face_index in range(6):
        driving = pressure_mid - pressure_near[face_index]
        if face_index == 4:
            driving = driving + lift_down
        if face_index == 5:
            driving = driving + lift_up
        flow_out = conductance[face_index] * driving
        change = change + jnp.maximum(flow_out, 0.0) * conc_mid + jnp.minimum(flow_out, 0.0) * conc_near[face_index]
    return conc_mid - solute_rate * change / (molten_state + 0.1)


def reference(thermal_undercool, mixture_alloying, fluid_fraction, kozeny_factor, state_marker):
    gravity = 4.0 / MESH_DEPTH_COUNT
    molten_state = jnp.where(state_marker == 1, 1.0, jnp.where(state_marker == 2, 0.0, fluid_fraction)).astype(jnp.float32)
    darcian_conductivity = kozeny_factor * (molten_state ** 3 / ((1.0 - molten_state) ** 2 + 0.25) + 0.02)
    forcing_amount = 2.0 * molten_state * (1.0 - molten_state) * thermal_undercool
    perm_ext = zero_rim(darcian_conductivity)
    alloying_content = mixture_alloying
    pressure = jnp.zeros_like(mixture_alloying)
    for time_step in range(STEPS):
        molten_mass_per_volume = 1.0 + 0.2 * alloying_content - 0.3 * thermal_undercool
        metal_head = gravity * (jnp.cumsum(molten_mass_per_volume, axis=2) - 0.5 * molten_mass_per_volume)
        coupling = face_terms(perm_ext, zero_rim(molten_mass_per_volume), gravity)
        pressure = metal_head
        for sweep_index in range(SWEEPS):
            pressure = jacobi_sweep(zero_rim(pressure), coupling, forcing_amount)
        alloying_content = solute_update(zero_rim(pressure), zero_rim(alloying_content), coupling, molten_state)
    return pressure, alloying_content
```

```python
import functools

import jax
import jax.numpy as jnp
from jax import lax
from jax.experimental import pallas as pl
from jax.experimental.pallas import tpu as pltpu
from jax.sharding import PartitionSpec as P

STEPS = 4
SWEEPS = 3
W = SWEEPS + 1
SOLUTE_RATE = 0.5
MESH = pl.DeviceIdType.MESH
GROUPS = 8
HALVES = 2
FIELDS = 4
LO = 12


def kernel(nx, nz, *refs):
    it = iter(refs)
    hbm = [next(it) for _ in range(5)]
    p_out, c_out = [next(it) for _ in range(2)]
    t_in, c_in, f_in, k_in, m_in = staged = [next(it) for _ in range(5)]
    o_pm, o_liq, strip = [next(it) for _ in range(3)]
    stat, cc, pa, pb, ra, rb, cr = [next(it) for _ in range(7)]
    axp, axm, ays, ayr, azp, azm, srcn, bb, gr, rh = [next(it) for _ in range(10)]
    cxp, cys, cyr, cz, lift, rl, tt = [next(it) for _ in range(7)]
    wts, hz, off, tt0 = [next(it) for _ in range(4)]
    xs, xr, zs, zr, es, er, ts, tr = [next(it) for _ in range(8)]
    sxs, sxr, szs, szr, ses, ser = [next(it) for _ in range(6)]
    send_sem, recv_sem, st_send, st_recv, in_sem = [next(it) for _ in range(5)]

    ny, n, lanes = t_in.shape
    wide = n + 2 * W
    per = lanes // GROUPS
    fine = stat.shape[2]
    mid = LO + W
    blocks = n // 8
    gravity = 4.0 / (nz * lanes)
    half = 0.5 * gravity
    ix, iz = lax.axis_index("gx"), lax.axis_index("gz")
    f32, bf16 = jnp.float32, jnp.bfloat16
    PERM, TEMP, LIQ, CONC = range(FIELDS)

    def inside(dx, dz):
        return (ix + dx >= 0) & (ix + dx < nx) & (iz + dz >= 0) & (iz + dz < nz)

    partners = [(dx, dz) for dz in range(-1, nz) for dx in (-1, 0, 1) if (dx, dz) != (0, 0)]

    def remote(src, dst, send, recv, dx, dz):
        return dx, dz, pltpu.make_async_remote_copy(
            src_ref=src, dst_ref=dst, send_sem=send, recv_sem=recv,
            device_id={"gx": ix + dx, "gz": iz + dz}, device_id_type=MESH)

    near = [(dx, dz) for dx, dz in partners if dz <= 1]

    def halo_copies(s):
        out = []
        for m, (dx, dz) in enumerate(near):
            a, b = (1, 0) if dx > 0 else (0, 1)
            side = 0 if dz > 0 else 1
            if dz == 0:
                src, dst = xs.at[s, a], xr.at[s, b]
            elif dx == 0:
                src, dst = zs.at[s], zr.at[s, side]
            else:
                src, dst = es.at[s, a], er.at[s, b, side]
            out.append(remote(src, dst, send_sem.at[s, m], recv_sem.at[s, m], dx, dz))
        return out

    def total_copies(s):
        below = [(dx, dz) for dx, dz in partners if dz > 0]
        return [remote(ts.at[s], tr.at[s, 1 - dx, dz - 1], send_sem.at[s, len(near) + m], recv_sem.at[s, len(near) + m],
                       dx, dz) for m, (dx, dz) in enumerate(below)]

    def static_copies(along_x):
        out = []
        for m, (dx, dz) in enumerate(near):
            a, b = (1, 0) if dx > 0 else (0, 1)
            side = 0 if dz > 0 else 1
            if dz == 0:
                src, dst = sxs.at[a], sxr.at[b]
            elif dx == 0:
                src, dst = szs, szr.at[side]
            else:
                src, dst = ses.at[a], ser.at[b, side]
            if (dz == 0) == along_x:
                out.append(remote(src, dst, st_send.at[m], st_recv.at[m], dx, dz))
        return out

    def start(copies):
        for dx, dz, c in copies:
            pl.when(inside(dx, dz))(c.start)

    def arrive(copies):
        for dx, dz, c in copies:
            pl.when(inside(-dx, -dz))(c.wait_recv)

    def sent(copies):
        for dx, dz, c in copies:
            pl.when(inside(dx, dz))(c.wait_send)

    loads = [pltpu.make_async_copy(a, b, in_sem.at[i]) for i, (a, b) in enumerate(zip(hbm, staged))]
    for load in loads:
        load.start()

    for ref in (xr, zr, er, tr, sxr, szr, ser):
        ref[...] = jnp.zeros_like(ref)
    barrier = pltpu.get_barrier_semaphore()
    count = 0
    for dx, dz in partners:
        @pl.when(inside(-dx, -dz))
        def _(dx=dx, dz=dz):
            pl.semaphore_signal(barrier, inc=1, device_id={"gx": ix - dx, "gz": iz - dz}, device_id_type=MESH)
        count = count + inside(dx, dz).astype(jnp.int32)

    def lane(rows):
        return lax.broadcasted_iota(jnp.int32, (rows, lanes), 1)

    def split(value):
        high = value.astype(bf16)
        low = (value - high.astype(f32)).astype(bf16)
        return jnp.concatenate([high, low], axis=1)

    r2 = lax.broadcasted_iota(jnp.int32, (2 * lanes, lanes), 0) % lanes
    c2 = lax.broadcasted_iota(jnp.int32, (2 * lanes, lanes), 1)
    same = (r2 // per) == (c2 // per)
    wts[0:2 * lanes] = jnp.where(same, jnp.where(r2 < c2, 1.0, 0.0), 0.0).astype(bf16)
    wts[2 * lanes:4 * lanes] = jnp.where(same, 1.0, 0.0).astype(bf16)

    zrows = jnp.zeros((8, lanes), f32)
    for h in range(HALVES):
        for z in range(fine):
            for r in (LO - 4, LO + wide - 4):
                stat[PERM, h, z, r:r + 8] = zrows
                pa[h, z + 1, r:r + 8] = zrows
                pb[h, z + 1, r:r + 8] = zrows

    for load in loads:
        load.wait()
    center = pl.ds(mid, n)
    window = pl.ds(LO, wide)
    top, bottom = pl.ds(LO, W), pl.ds(mid + n, W)

    ln = lane(n)
    packed = [jnp.zeros((n, lanes), f32)] * FIELDS
    for y in range(ny):
        mark, t, c = m_in[y], t_in[y], c_in[y]
        liq = jnp.where(mark == 1, 1.0, jnp.where(mark == 2, 0.0, f_in[y]))
        solid = 1.0 - liq
        pm = k_in[y] * (liq * liq * liq / (solid * solid + 0.25) + 0.02)
        o_pm[y] = pm
        o_liq[y] = liq
        for f, v in enumerate((pm, t, liq, c)):
            strip[f, y, 0:W] = v[0:W]
            strip[f, y, W:2 * W] = v[n - W:n]
            packed[f] = jnp.where(ln // (2 * W) == y, pltpu.roll(v, (y * 2 * W + W) % lanes, 1), packed[f])
    for f in range(FIELDS):
        szs[f] = packed[f]
        ses[0, f] = packed[f][0:W]
        ses[1, f] = packed[f][n - W:n]
    pl.semaphore_wait(barrier, count)
    start(static_copies(False))

    def spread(get, put, rows):
        lw = lane(rows)
        res, grp, zc = (lw + W) % fine, lw // per, lw % per
        for h in range(HALVES):
            vals = [get(HALVES * g + h) for g in range(GROUPS)]
            moved = []
            for d in range(fine):
                comb = vals[0]
                for g in range(1, GROUPS):
                    comb = jnp.where(res == (g + d) % fine, vals[g], comb)
                z = fine * zc + (grp + d) % fine - W
                moved.append(jnp.take_along_axis(comb, jnp.clip(z, 0, lanes - 1), axis=1, mode="promise_in_bounds"))
            for z in range(fine):
                v = moved[z]
                for g in range(1, GROUPS):
                    v = jnp.where(grp == g, moved[(z - g) % fine], v)
                zw = fine * zc + z
                put(h, z, jnp.where((zw >= W) & (zw < W + lanes), v, 0.0))

    def gathered(get, put, rows):
        lw = lane(rows)
        res, grp = (lw + W) % fine, lw // per
        for h in range(HALVES):
            vals = [get(h, z) for z in range(fine)]
            moved = []
            for d in range(fine):
                comb = vals[d]
                for g in range(1, GROUPS):
                    comb = jnp.where(grp == g, vals[(g + d) % fine], comb)
                g = jnp.minimum((res - d + fine) % fine, GROUPS - 1)
                moved.append(jnp.take_along_axis(comb, g * per + (lw + W) // fine, axis=1, mode="promise_in_bounds"))
            for g in range(GROUPS):
                v = moved[0]
                for d in range(1, fine):
                    v = jnp.where(res == (g + d) % fine, moved[d], v)
                put(HALVES * g + h, v)

    for f in range(FIELDS):
        def put(h, z, v, f=f):
            sxs[0, f, h, z] = v[0:W]
            sxs[1, f, h, z] = v[W:2 * W]
        spread(lambda y, f=f: strip[f, y], put, 2 * W)
    start(static_copies(True))

    def cells(f):
        return cc.at[0] if f == CONC else stat.at[f]

    for f, ref in ((CONC, c_in), (TEMP, t_in), (PERM, o_pm), (LIQ, o_liq)):
        for r in range(0, n, 16):
            def put(h, z, v, f=f, r=r):
                cells(f)[h, z, mid + r:mid + r + 16, :] = v
            spread(lambda y, ref=ref, r=r: ref[y, r:r + 16], put, 16)

    def own_sum(values):
        zc = lane(n) % per
        out = jnp.zeros((n, lanes), f32)
        for first in sorted({0, W % fine, (W + lanes) % fine}):
            last = min([e for e in (W % fine, (W + lanes) % fine, fine) if e > first])
            part = values[first]
            for z in range(first + 1, last):
                part = part + values[z]
            zw = fine * zc + first
            out = out + jnp.where((zw >= W) & (zw < W + lanes), part, 0.0)
        return out

    def send_totals(s, sums):
        both = jnp.concatenate([split(tt0[h] + 0.2 * sums[h]) for h in range(HALVES)], axis=0)
        tot = jnp.dot(both, wts[2 * lanes:4 * lanes], preferred_element_type=f32)
        slot = lane(8) % per
        out = jnp.zeros((8, lanes), f32)
        for i in range(HALVES * blocks):
            out = jnp.where(slot == i, tot[8 * i:8 * i + 8], out)
        ts[s] = out
        start(total_copies(s))

    def edge(h, rows):
        return lane(rows) < per if h == 0 else lane(rows) >= lanes - per

    shift = (per, lanes - per)

    def turn(s):
        for h in range(HALVES):
            for z in range(fine):
                cr[h, z] = jnp.where(edge(h, n), 0.0, pltpu.roll(cc[s, 1 - h, z, center, :], shift[h], 1))

    for h in range(HALVES):
        tt0[h] = own_sum([1.0 - 0.3 * stat[TEMP, h, z, center, :] for z in range(fine)])
    send_totals(0, [own_sum([cc[0, h, z, center, :] for z in range(fine)]) for h in range(HALVES)])
    turn(0)

    zc_w = lane(wide) % per

    def insert(dst, strips, packed):
        for h in range(HALVES):
            for z in range(fine):
                dst[h, z, top, :] = strips(0, h, z)
                dst[h, z, bottom, :] = strips(1, h, z)
            for k in range(2 * W):
                at, z = divmod(k if k < W else lanes + k, fine)
                moved = pltpu.roll(packed, (at - h * 2 * W - k) % lanes, 1)
                dst[h, z, window, :] = jnp.where(zc_w == at, moved, dst[h, z, window, :])

    k_n, k_e = lane(n) % (2 * W), lane(W) % (2 * W)

    arrive(static_copies(False))
    arrive(static_copies(True))
    for f in range(FIELDS):
        hz[0:W] = jnp.where(k_e < W, ser[0, 0, f], ser[0, 1, f])
        hz[W:W + n] = jnp.where(k_n < W, szr[0, f], szr[1, f])
        hz[W + n:wide] = jnp.where(k_e < W, ser[1, 0, f], ser[1, 1, f])
        insert(cells(f), lambda b, h, z, f=f: sxr[b, f, h, z], hz[...])

    up_rows, down_rows = pl.ds(LO + 1, wide), pl.ds(LO - 1, wide)
    for h in range(HALVES):
        for z in range(fine):
            pm = stat[PERM, h, z, window, :]
            over = stat[PERM, h, z + 1, window, :] if z < fine - 1 else pltpu.roll(stat[PERM, h, 0, window, :], lanes - 1, 1)
            under = stat[PERM, h, z - 1, window, :] if z > 0 else pltpu.roll(stat[PERM, h, fine - 1, window, :], 1, 1)
            cross = jnp.where(edge(h, wide), 0.0, pltpu.roll(stat[PERM, 1 - h, z, window, :], shift[h], 1))
            c = [0.5 * (pm + other) for other in (
                stat[PERM, h, z, up_rows, :], stat[PERM, h, z, down_rows, :], stat[PERM, 1 - h, z, window, :], cross, over, under)]
            total = c[0] + c[1] + c[2] + c[3] + c[4] + c[5]
            real = pm > 0.0
            inv = jnp.where(real, 1.0 / jnp.where(real, total, 1.0), 0.0)
            cxp[h, z, window, :] = c[0]
            if h == 0:
                cys[z, window, :] = c[2]
            cyr[h, z, window, :] = c[3]
            cz[h, z + 1, window, :] = c[4]
            if z == 0:
                cz[h, 0, window, :] = c[5]
            axp[h, z] = c[0] * inv
            axm[h, z] = c[1] * inv
            ays[h, z] = c[2] * inv
            ayr[h, z] = jnp.where(edge(h, wide), 0.0, c[3] * inv)
            azp[h, z] = c[4] * inv
            azm[h, z] = c[5] * inv
            liq, t = stat[LIQ, h, z, window, :], stat[TEMP, h, z, window, :]
            srcn[h, z] = 2.0 * liq * (1.0 - liq) * t * inv
            tt[h, z] = jnp.where(real, 1.0 - 0.3 * t, 0.0)
            gr[h, z] = jnp.where(real, gravity, 0.0)
            zw = fine * (lane(n) % per) + z
            rl[h, z] = jnp.where((zw >= W) & (zw < W + lanes), SOLUTE_RATE / (stat[LIQ, h, z, center, :] + 0.1), 0.0)

    def keep(p, r, h, z, v):
        p[h, z + 1, window, :] = v
        r[1 - h, z] = pltpu.roll(v, shift[1 - h], 1)
        if z == 0:
            p[h, fine + 1, window, :] = pltpu.roll(v, lanes - 1, 1)
        if z == fine - 1:
            p[h, 0, window, :] = pltpu.roll(v, 1, 1)

    order = [0, fine - 1] + list(range(1, fine - 1))

    def carried(flow, own, other):
        return flow * jnp.where(flow > 0.0, own, other)

    up_c, down_c = pl.ds(mid + 1, n), pl.ds(mid - 1, n)

    def step(s, final):
        if not isinstance(s, int) or s > 0:
            arrive(halo_copies(s))
            hz[0:W] = jnp.where(k_e < W, er[s, 0, 0], er[s, 0, 1])
            hz[W:W + n] = jnp.where(k_n < W, zr[s, 0], zr[s, 1])
            hz[W + n:wide] = jnp.where(k_e < W, er[s, 1, 0], er[s, 1, 1])
            insert(cc.at[s], lambda b, h, z: xr[s, b, h, z], hz[...])
        sums = []
        for h in range(HALVES):
            for z in range(fine):
                rh[h, z] = tt[h, z] + 0.2 * cc[s, h, z, window, :]
            before = rh[h, 0]
            for z in range(1, W):
                before = before + rh[h, z]
            run = jnp.where(zc_w == 0, -before, 0.0)
            for z in range(fine):
                rho = rh[h, z]
                pa[h, z + 1, window, :] = run + 0.5 * rho
                run = run + rho
            sums.append(run)
            lo = half * (pltpu.roll(rh[h, fine - 1], 1, 1) + rh[h, 0])
            lift[h, 0, window, :] = lo
            for z in range(fine):
                other = rh[h, z + 1] if z < fine - 1 else pltpu.roll(rh[h, 0], lanes - 1, 1)
                hi = half * (rh[h, z] + other)
                lift[h, z + 1, window, :] = hi
                bb[h, z] = srcn[h, z] - azp[h, z] * hi + azm[h, z] * lo
                lo = hi
        arrive(total_copies(s))
        total = [tr[s, side, 0] for side in range(3)]
        for d in range(1, nz - 1):
            total = [total[side] + tr[s, side, d] for side in range(3)]
        slot = lane(8) % per
        for h in range(HALVES):
            off[h, 0:W] = jnp.where(slot == h * blocks + blocks - 1, total[0], 0.0)[8 - W:8]
            for j in range(blocks):
                off[h, W + 8 * j:W + 8 * j + 8] = jnp.where(slot == h * blocks + j, total[1], 0.0)
            off[h, W + n:wide] = jnp.where(slot == h * blocks, total[2], 0.0)[0:W]
        both = jnp.concatenate([jnp.concatenate([split(sums[h]), split(off[h])], axis=1) for h in range(HALVES)], axis=0)
        above = jnp.dot(both, wts[...], preferred_element_type=f32)
        for z in order:
            for h in range(HALVES):
                keep(pa, ra, h, z, gr[h, z] * (pa[h, z + 1, window, :] + above[h * wide:(h + 1) * wide]))

        old, new, rold, rnew = pa, pb, ra, rb
        for sweep in range(SWEEPS):
            for z in order:
                for h in range(HALVES):
                    v = bb[h, z] + axp[h, z] * old[h, z + 1, up_rows, :] + axm[h, z] * old[h, z + 1, down_rows, :]
                    v = v + (ays[h, z] * old[1 - h, z + 1, window, :] + ayr[h, z] * rold[h, z])
                    v = v + (azp[h, z] * old[h, z + 2, window, :] + azm[h, z] * old[h, z, window, :])
                    keep(new, rnew, h, z, v)
            old, new, rold, rnew = new, old, rnew, rold

        slab = jnp.zeros((n, lanes), f32)
        k_slab = lane(n) % per
        fresh_all = [[], []]
        wrap = [(pltpu.roll(cc[s, h, fine - 1, center, :], 1, 1), pltpu.roll(cc[s, h, 0, center, :], lanes - 1, 1))
                for h in range(HALVES)]
        low = [carried(cz[h, 0, center, :] * (old[h, 0, center, :] - old[h, 1, center, :] + lift[h, 0, center, :]),
                       wrap[h][0], cc[s, h, 0, center, :]) for h in range(HALVES)]
        inner = pl.ds(W, n)
        for z in range(fine):
            ps = [old[h, z + 1, center, :] for h in range(HALVES)]
            cs = [cc[s, h, z, center, :] for h in range(HALVES)]
            between = carried(cys[z, center, :] * (ps[0] - ps[1]), cs[0], cs[1])
            for h in range(HALVES):
                p, c = ps[h], cs[h]
                change = carried(cxp[h, z, center, :] * (p - old[h, z + 1, up_c, :]), c, cc[s, h, z, up_c, :])
                change = change + carried(cxp[h, z, down_c, :] * (p - old[h, z + 1, down_c, :]), c, cc[s, h, z, down_c, :])
                side = jnp.where(edge(h, n), 0.0, rold[h, z, inner, :])
                change = change + carried(cyr[h, z, center, :] * (p - side), c, cr[h, z])
                change = change + between if h == 0 else change - between
                over = cc[s, h, z + 1, center, :] if z < fine - 1 else wrap[h][1]
                high = carried(cz[h, z + 1, center, :] * (p - old[h, z + 2, center, :] + lift[h, z + 1, center, :]), c, over)
                change = change + (high - low[h])
                low[h] = high
                fresh = c - rl[h, z] * change
                cc[s + 1, h, z, center, :] = fresh
                if not final:
                    xs[s + 1, 0, h, z] = fresh[0:W]
                    xs[s + 1, 1, h, z] = fresh[n - W:n]
                    for j in range(2 * W):
                        at, zj = divmod(lanes + j if j < W else j, fine)
                        if zj == z:
                            k = h * 2 * W + j
                            slab = jnp.where(k_slab == k, pltpu.roll(fresh, (k - at) % lanes, 1), slab)
        if not final:
            zs[s + 1] = slab
            es[s + 1, 0] = slab[0:W]
            es[s + 1, 1] = slab[n - W:n]
            start(halo_copies(s + 1))
            send_totals(s + 1, [own_sum([cc[s + 1, h, z, center, :] for z in range(fine)]) for h in range(HALVES)])
            turn(s + 1)
        else:
            for r in range(0, n, 16):
                def put_p(y, v, r=r):
                    p_out[y, r:r + 16] = v

                def put_c(y, v, r=r):
                    c_out[y, r:r + 16] = v
                gathered(lambda h, z, r=r: old[h, z + 1, mid + r:mid + r + 16, :], put_p, 16)
                gathered(lambda h, z, r=r: cc[s + 1, h, z, mid + r:mid + r + 16, :], put_c, 16)

    for s in range(STEPS):
        step(s, s == STEPS - 1)

    sent(static_copies(False))
    sent(static_copies(True))
    for s in range(STEPS):
        if s > 0:
            sent(halo_copies(s))
        sent(total_copies(s))


def on_device(nx, nz, *args):
    ny, n, lanes = args[0].shape
    wide = n + 2 * W
    rows = wide + 2 * LO
    per = lanes // GROUPS
    fine = -(-(lanes + 2 * W) // per)
    copies = 8 + 3 * (nz - 1)

    def vmem(*shape):
        return pltpu.VMEM(shape, jnp.float32)

    padded, plain, own = (HALVES, fine, rows, lanes), (HALVES, fine, wide, lanes), (HALVES, fine, n, lanes)
    slots = (HALVES, fine + 2, rows, lanes)
    scratch = [pltpu.VMEM((ny, n, lanes), a.dtype) for a in args]
    scratch += [vmem(ny, n, lanes)] * 2 + [vmem(FIELDS, ny, 2 * W, lanes)]
    scratch += [vmem(FIELDS - 1, *padded), vmem(STEPS + 1, *padded), vmem(*slots), vmem(*slots)]
    scratch += [vmem(*plain), vmem(*plain), vmem(*own)]
    scratch += [vmem(*plain)] * 10
    scratch += [vmem(*padded), vmem(fine, rows, lanes), vmem(*padded), vmem(HALVES, fine + 1, rows, lanes),
                vmem(HALVES, fine + 1, rows, lanes), vmem(*own), vmem(*plain)]
    scratch += [pltpu.VMEM((4 * lanes, lanes), jnp.bfloat16), vmem(wide, lanes), vmem(HALVES, wide, lanes),
                vmem(HALVES, n, lanes)]
    scratch += [vmem(STEPS, 2, HALVES, fine, W, lanes)] * 2
    scratch += [vmem(STEPS, n, lanes), vmem(STEPS, 2, n, lanes)]
    scratch += [vmem(STEPS, 2, W, lanes), vmem(STEPS, 2, 2, W, lanes)]
    scratch += [vmem(STEPS, 8, lanes), vmem(STEPS, 3, nz - 1, 8, lanes)]
    scratch += [vmem(2, FIELDS, HALVES, fine, W, lanes)] * 2
    scratch += [vmem(FIELDS, n, lanes), vmem(2, FIELDS, n, lanes), vmem(2, FIELDS, W, lanes), vmem(2, 2, FIELDS, W, lanes)]
    scratch += [pltpu.SemaphoreType.DMA((STEPS, copies))] * 2 + [pltpu.SemaphoreType.DMA((8,))] * 2
    scratch += [pltpu.SemaphoreType.DMA((5,))]
    return tuple(pl.pallas_call(
        functools.partial(kernel, nx, nz),
        out_shape=[jax.ShapeDtypeStruct((ny, n, lanes), jnp.float32)] * 2,
        in_specs=[pl.BlockSpec(memory_space=pltpu.HBM)] * 5,
        out_specs=[pl.BlockSpec(memory_space=pltpu.VMEM)] * 2,
        scratch_shapes=scratch,
        compiler_params=pltpu.CompilerParams(
            collective_id=0, has_side_effects=True, vmem_limit_bytes=63 * 1024 * 1024),
    )(*args))


def solution(mesh):
    placed = P(None, "gx", "gz")
    return jax.shard_map(
        functools.partial(on_device, mesh.shape["gx"], mesh.shape["gz"]),
        mesh=mesh,
        in_specs=(placed,) * 5,
        out_specs=(placed, placed),
        check_vma=False,
    )
```

```python
import functools

import jax
import jax.numpy as jnp
from jax import lax
from jax.experimental import pallas as pl
from jax.experimental.pallas import tpu as pltpu
from jax.sharding import PartitionSpec as P

STEPS = 4
SWEEPS = 3
W = SWEEPS + 1
SOLUTE_RATE = 0.5
MESH = pl.DeviceIdType.MESH
GROUPS = 8
HALVES = 2
FIELDS = 4
LO = 12
PART = 16


def kernel(nx, nz, *refs):
    it = iter(refs)
    hbm = [next(it) for _ in range(5)]
    p_out, c_out = [next(it) for _ in range(2)]
    t_in, c_in, f_in, k_in, m_in = staged = [next(it) for _ in range(5)]
    o_pm, o_liq, strip = [next(it) for _ in range(3)]
    stat, cc, pa, pb, ra, rb, cr = [next(it) for _ in range(7)]
    axp, axm, ays, ayr, azp, azm, srcn, bb, gr, rh = [next(it) for _ in range(10)]
    cxp, cys, cyr, cz, lift, rl, tt = [next(it) for _ in range(7)]
    wts, hz, off, tt0 = [next(it) for _ in range(4)]
    xs, xr, zs, zr, es, er, ts, tr = [next(it) for _ in range(8)]
    sxs, sxr, szs, szr, ses, ser = [next(it) for _ in range(6)]
    send_sem, recv_sem, st_send, st_recv, in_sem, out_sem = [next(it) for _ in range(6)]

    ny, n, lanes = t_in.shape
    wide = n + 2 * W
    per = lanes // GROUPS
    fine = stat.shape[2]
    mid = LO + W
    blocks = n // 8
    gravity = 4.0 / (nz * lanes)
    half = 0.5 * gravity
    ix, iz = lax.axis_index("gx"), lax.axis_index("gz")
    f32, bf16 = jnp.float32, jnp.bfloat16
    PERM, TEMP, LIQ, CONC = range(FIELDS)

    def inside(dx, dz):
        return (ix + dx >= 0) & (ix + dx < nx) & (iz + dz >= 0) & (iz + dz < nz)

    partners = [(dx, dz) for dz in range(-1, nz) for dx in (-1, 0, 1) if (dx, dz) != (0, 0)]

    def remote(src, dst, send, recv, dx, dz):
        return dx, dz, pltpu.make_async_remote_copy(
            src_ref=src, dst_ref=dst, send_sem=send, recv_sem=recv,
            device_id={"gx": ix + dx, "gz": iz + dz}, device_id_type=MESH)

    near = [(dx, dz) for dx, dz in partners if dz <= 1]

    def halo_copies(s, along_x):
        out = []
        for m, (dx, dz) in enumerate(near):
            a, b = (1, 0) if dx > 0 else (0, 1)
            side = 0 if dz > 0 else 1
            if dz == 0:
                src, dst = xs.at[s, a], xr.at[s, b]
            elif dx == 0:
                src, dst = zs.at[s], zr.at[s, side]
            else:
                src, dst = es.at[s, a], er.at[s, b, side]
            if (dx != 0) == along_x:
                out.append(remote(src, dst, send_sem.at[s, m], recv_sem.at[s, m], dx, dz))
        return sorted(out, key=lambda item: item[1] != 0)

    def total_copies(s):
        below = [(dx, dz) for dx, dz in partners if dz > 0]
        return [remote(ts.at[s], tr.at[s, 1 - dx, dz - 1], send_sem.at[s, len(near) + m], recv_sem.at[s, len(near) + m],
                       dx, dz) for m, (dx, dz) in enumerate(below)]

    def static_copies(along_x):
        out = []
        for m, (dx, dz) in enumerate(near):
            a, b = (1, 0) if dx > 0 else (0, 1)
            side = 0 if dz > 0 else 1
            if dz == 0:
                src, dst = sxs.at[a], sxr.at[b]
            elif dx == 0:
                src, dst = szs, szr.at[side]
            else:
                src, dst = ses.at[a], ser.at[b, side]
            if (dx != 0) == along_x:
                out.append(remote(src, dst, st_send.at[m], st_recv.at[m], dx, dz))
        return sorted(out, key=lambda item: item[1] != 0)

    def start(copies):
        for dx, dz, c in copies:
            pl.when(inside(dx, dz))(c.start)

    def arrive(copies):
        for dx, dz, c in copies:
            pl.when(inside(-dx, -dz))(c.wait_recv)

    def sent(copies):
        for dx, dz, c in copies:
            pl.when(inside(dx, dz))(c.wait_send)

    loads = [pltpu.make_async_copy(a, b, in_sem.at[i]) for i, (a, b) in enumerate(zip(hbm, staged))]
    for load in loads:
        load.start()

    for ref in (xr, zr, er, tr, sxr, szr, ser):
        ref[...] = jnp.zeros_like(ref)
    barrier = pltpu.get_barrier_semaphore()
    count = 0
    for dx, dz in partners:
        @pl.when(inside(-dx, -dz))
        def _(dx=dx, dz=dz):
            pl.semaphore_signal(barrier, inc=1, device_id={"gx": ix - dx, "gz": iz - dz}, device_id_type=MESH)
        count = count + inside(dx, dz).astype(jnp.int32)

    def lane(rows):
        return lax.broadcasted_iota(jnp.int32, (rows, lanes), 1)

    def split(value):
        high = value.astype(bf16)
        low = (value - high.astype(f32)).astype(bf16)
        return jnp.concatenate([high, low], axis=1)

    r2 = lax.broadcasted_iota(jnp.int32, (2 * lanes, lanes), 0) % lanes
    c2 = lax.broadcasted_iota(jnp.int32, (2 * lanes, lanes), 1)
    same = (r2 // per) == (c2 // per)
    wts[0:2 * lanes] = jnp.where(same, jnp.where(r2 < c2, 1.0, 0.0), 0.0).astype(bf16)
    wts[2 * lanes:4 * lanes] = jnp.where(same, 1.0, 0.0).astype(bf16)

    zrows = jnp.zeros((8, lanes), f32)
    for h in range(HALVES):
        for z in range(fine):
            for r in (LO - 4, LO + wide - 4):
                stat[PERM, h, z, r:r + 8] = zrows
                pa[h, z + 1, r:r + 8] = zrows
                pb[h, z + 1, r:r + 8] = zrows

    for load in loads:
        load.wait()
    center = pl.ds(mid, n)
    window = pl.ds(LO, wide)
    top, bottom = pl.ds(LO, W), pl.ds(mid + n, W)

    ln = lane(n)
    packed = [jnp.zeros((n, lanes), f32)] * FIELDS
    for y in range(ny):
        mark, t, c = m_in[y], t_in[y], c_in[y]
        liq = jnp.where(mark == 1, 1.0, jnp.where(mark == 2, 0.0, f_in[y]))
        solid = 1.0 - liq
        pm = k_in[y] * (liq * liq * liq / (solid * solid + 0.25) + 0.02)
        o_pm[y] = pm
        o_liq[y] = liq
        for f, v in enumerate((pm, t, liq, c)):
            strip[f, y, 0:W] = v[0:W]
            strip[f, y, W:2 * W] = v[n - W:n]
            packed[f] = jnp.where(ln // (2 * W) == y, pltpu.roll(v, (y * 2 * W + W) % lanes, 1), packed[f])
    for f in range(FIELDS):
        szs[f] = packed[f]
        ses[0, f] = packed[f][0:W]
        ses[1, f] = packed[f][n - W:n]
    pl.semaphore_wait(barrier, count)
    start(static_copies(False))

    def spread(get, put, rows):
        lw = lane(rows)
        res, grp, zc = (lw + W) % fine, lw // per, lw % per
        for h in range(HALVES):
            vals = [get(HALVES * g + h) for g in range(GROUPS)]
            moved = []
            for d in range(fine):
                comb = vals[0]
                for g in range(1, GROUPS):
                    comb = jnp.where(res == (g + d) % fine, vals[g], comb)
                z = fine * zc + (grp + d) % fine - W
                moved.append(jnp.take_along_axis(comb, jnp.clip(z, 0, lanes - 1), axis=1, mode="promise_in_bounds"))
            for z in range(fine):
                v = moved[z]
                for g in range(1, GROUPS):
                    v = jnp.where(grp == g, moved[(z - g) % fine], v)
                zw = fine * zc + z
                put(h, z, jnp.where((zw >= W) & (zw < W + lanes), v, 0.0))

    for f in range(FIELDS):
        def put(h, z, v, f=f):
            sxs[0, f, h, z] = v[0:W]
            sxs[1, f, h, z] = v[W:2 * W]
        spread(lambda y, f=f: strip[f, y], put, 2 * W)
    start(static_copies(True))

    def cells(f):
        return cc.at[0] if f == CONC else stat.at[f]

    for f, ref in ((CONC, c_in), (TEMP, t_in), (PERM, o_pm), (LIQ, o_liq)):
        for r in range(0, n, 16):
            def put(h, z, v, f=f, r=r):
                cells(f)[h, z, mid + r:mid + r + 16, :] = v
            spread(lambda y, ref=ref, r=r: ref[y, r:r + 16], put, 16)

    def own_sum(values):
        zc = lane(n) % per
        out = jnp.zeros((n, lanes), f32)
        for first in sorted({0, W % fine, (W + lanes) % fine}):
            last = min([e for e in (W % fine, (W + lanes) % fine, fine) if e > first])
            part = values[first]
            for z in range(first + 1, last):
                part = part + values[z]
            zw = fine * zc + first
            out = out + jnp.where((zw >= W) & (zw < W + lanes), part, 0.0)
        return out

    def send_totals(s, sums):
        both = jnp.concatenate([split(tt0[h] + 0.2 * sums[h]) for h in range(HALVES)], axis=0)
        tot = jnp.dot(both, wts[2 * lanes:4 * lanes], preferred_element_type=f32)
        slot = lane(8) % per
        out = jnp.zeros((8, lanes), f32)
        for i in range(HALVES * blocks):
            out = jnp.where(slot == i, tot[8 * i:8 * i + 8], out)
        ts[s] = out
        start(total_copies(s))

    def edge(h, rows):
        return lane(rows) < per if h == 0 else lane(rows) >= lanes - per

    shift = (per, lanes - per)

    def turn(s):
        for h in range(HALVES):
            for z in range(fine):
                cr[h, z] = jnp.where(edge(h, n), 0.0, pltpu.roll(cc[s, 1 - h, z, center, :], shift[h], 1))

    for h in range(HALVES):
        tt0[h] = own_sum([1.0 - 0.3 * stat[TEMP, h, z, center, :] for z in range(fine)])
    send_totals(0, [own_sum([cc[0, h, z, center, :] for z in range(fine)]) for h in range(HALVES)])
    turn(0)

    zc_w = lane(wide) % per

    def insert(dst, packed, row, rows):
        zc, at_rows = lane(rows) % per, pl.ds(LO + row, rows)
        for h in range(HALVES):
            for k in range(2 * W):
                at, z = divmod(k if k < W else lanes + k, fine)
                moved = pltpu.roll(packed, (at - h * 2 * W - k) % lanes, 1)
                dst[h, z, at_rows, :] = jnp.where(zc == at, moved, dst[h, z, at_rows, :])

    def insert_strips(dst, strips, corners):
        for h in range(HALVES):
            for z in range(fine):
                dst[h, z, top, :] = strips(0, h, z)
                dst[h, z, bottom, :] = strips(1, h, z)
        for b in range(2):
            hz[b] = jnp.where(k_e < W, corners(b, 0), corners(b, 1))
            insert(dst, hz[b], b * (n + W), W)

    k_n, k_e = lane(n) % (2 * W), lane(W) % (2 * W)

    arrive(static_copies(False))
    for f in range(FIELDS):
        insert(cells(f), jnp.where(k_n < W, szr[0, f], szr[1, f]), W, n)

    up_rows, down_rows = pl.ds(LO + 1, wide), pl.ds(LO - 1, wide)

    def coefficients(row, rows):
        here, up, down, flat = pl.ds(LO + row, rows), pl.ds(LO + row + 1, rows), pl.ds(LO + row - 1, rows), pl.ds(row, rows)
        beside = [edge(h, rows) for h in range(HALVES)]
        for h in range(HALVES):
            for z in range(fine):
                pm = stat[PERM, h, z, here, :]
                over = stat[PERM, h, z + 1, here, :] if z < fine - 1 else pltpu.roll(stat[PERM, h, 0, here, :], lanes - 1, 1)
                under = stat[PERM, h, z - 1, here, :] if z > 0 else pltpu.roll(stat[PERM, h, fine - 1, here, :], 1, 1)
                cross = jnp.where(beside[h], 0.0, pltpu.roll(stat[PERM, 1 - h, z, here, :], shift[h], 1))
                c = [0.5 * (pm + other) for other in (
                    stat[PERM, h, z, up, :], stat[PERM, h, z, down, :], stat[PERM, 1 - h, z, here, :], cross, over, under)]
                total = c[0] + c[1] + c[2] + c[3] + c[4] + c[5]
                real = pm > 0.0
                inv = jnp.where(real, 1.0 / jnp.where(real, total, 1.0), 0.0)
                cxp[h, z, here, :] = c[0]
                if h == 0:
                    cys[z, here, :] = c[2]
                cyr[h, z, here, :] = c[3]
                cz[h, z + 1, here, :] = c[4]
                if z == 0:
                    cz[h, 0, here, :] = c[5]
                axp[h, z, flat] = c[0] * inv
                axm[h, z, flat] = c[1] * inv
                ays[h, z, flat] = c[2] * inv
                ayr[h, z, flat] = jnp.where(beside[h], 0.0, c[3] * inv)
                azp[h, z, flat] = c[4] * inv
                azm[h, z, flat] = c[5] * inv
                liq, t = stat[LIQ, h, z, here, :], stat[TEMP, h, z, here, :]
                srcn[h, z, flat] = 2.0 * liq * (1.0 - liq) * t * inv
                tt[h, z, flat] = jnp.where(real, 1.0 - 0.3 * t, 0.0)
                gr[h, z, flat] = jnp.where(real, gravity, 0.0)

    zc_n = lane(n) % per
    for h in range(HALVES):
        for z in range(fine):
            zw = fine * zc_n + z
            rl[h, z] = jnp.where((zw >= W) & (zw < W + lanes), SOLUTE_RATE / (stat[LIQ, h, z, center, :] + 0.1), 0.0)
    coefficients(8, wide - 16)
    sent(static_copies(False))
    arrive(static_copies(True))
    for f in range(FIELDS):
        insert_strips(cells(f), lambda b, h, z, f=f: sxr[b, f, h, z], lambda b, side, f=f: ser[b, side, f])
    for row in (0, wide - 8):
        coefficients(row, 8)
    sent(static_copies(True))

    def keep(p, r, h, z, v):
        p[h, z + 1, window, :] = v
        r[1 - h, z] = pltpu.roll(v, shift[1 - h], 1)
        if z == 0:
            p[h, fine + 1, window, :] = pltpu.roll(v, lanes - 1, 1)
        if z == fine - 1:
            p[h, 0, window, :] = pltpu.roll(v, 1, 1)

    order = [0, fine - 1] + list(range(1, fine - 1))

    def carried(flow, own, other):
        return flow * jnp.where(flow > 0.0, own, other)

    def step(s, final):
        if s > 0:
            sent(halo_copies(s, True))
            sent(halo_copies(s, False))
            sent(total_copies(s))
            arrive(halo_copies(s, False))
            insert(cc.at[s], jnp.where(k_n < W, zr[s, 0], zr[s, 1]), W, n)
            arrive(halo_copies(s, True))
            insert_strips(cc.at[s], lambda b, h, z: xr[s, b, h, z], lambda b, side: er[s, b, side])
        sums = []
        for h in range(HALVES):
            for z in range(fine):
                rh[h, z] = tt[h, z] + 0.2 * cc[s, h, z, window, :]
            before = rh[h, 0]
            for z in range(1, W):
                before = before + rh[h, z]
            run = jnp.where(zc_w == 0, -before, 0.0)
            for z in range(fine):
                rho = rh[h, z]
                pa[h, z + 1, window, :] = run + 0.5 * rho
                run = run + rho
            sums.append(run)
            lo = half * (pltpu.roll(rh[h, fine - 1], 1, 1) + rh[h, 0])
            lift[h, 0, window, :] = lo
            for z in range(fine):
                other = rh[h, z + 1] if z < fine - 1 else pltpu.roll(rh[h, 0], lanes - 1, 1)
                hi = half * (rh[h, z] + other)
                lift[h, z + 1, window, :] = hi
                bb[h, z] = srcn[h, z] - azp[h, z] * hi + azm[h, z] * lo
                lo = hi
        if s == 0:
            sent(total_copies(0))
        arrive(total_copies(s))
        total = [tr[s, side, 0] for side in range(3)]
        for d in range(1, nz - 1):
            total = [total[side] + tr[s, side, d] for side in range(3)]
        slot = lane(8) % per
        for h in range(HALVES):
            off[h, 0:W] = jnp.where(slot == h * blocks + blocks - 1, total[0], 0.0)[8 - W:8]
            for j in range(blocks):
                off[h, W + 8 * j:W + 8 * j + 8] = jnp.where(slot == h * blocks + j, total[1], 0.0)
            off[h, W + n:wide] = jnp.where(slot == h * blocks, total[2], 0.0)[0:W]
        both = jnp.concatenate([jnp.concatenate([split(sums[h]), split(off[h])], axis=1) for h in range(HALVES)], axis=0)
        above = jnp.dot(both, wts[...], preferred_element_type=f32)
        for z in order:
            for h in range(HALVES):
                keep(pa, ra, h, z, gr[h, z] * (pa[h, z + 1, window, :] + above[h * wide:(h + 1) * wide]))

        old, new, rold, rnew = pa, pb, ra, rb
        for sweep in range(SWEEPS):
            for z in order:
                for h in range(HALVES):
                    v = bb[h, z] + axp[h, z] * old[h, z + 1, up_rows, :] + axm[h, z] * old[h, z + 1, down_rows, :]
                    v = v + (ays[h, z] * old[1 - h, z + 1, window, :] + ayr[h, z] * rold[h, z])
                    v = v + (azp[h, z] * old[h, z + 2, window, :] + azm[h, z] * old[h, z, window, :])
                    keep(new, rnew, h, z, v)
            old, new, rold, rnew = new, old, rnew, rold

        def transport(row, rows):
            here, up, down = pl.ds(mid + row, rows), pl.ds(mid + row + 1, rows), pl.ds(mid + row - 1, rows)
            flat, inner = pl.ds(row, rows), pl.ds(W + row, rows)
            slab = jnp.zeros((rows, lanes), f32)
            k_slab = lane(rows) % per
            wrap = [(pltpu.roll(cc[s, h, fine - 1, here, :], 1, 1), pltpu.roll(cc[s, h, 0, here, :], lanes - 1, 1))
                    for h in range(HALVES)]
            low = [carried(cz[h, 0, here, :] * (old[h, 0, here, :] - old[h, 1, here, :] + lift[h, 0, here, :]),
                           wrap[h][0], cc[s, h, 0, here, :]) for h in range(HALVES)]
            for z in range(fine):
                ps = [old[h, z + 1, here, :] for h in range(HALVES)]
                cs = [cc[s, h, z, here, :] for h in range(HALVES)]
                between = carried(cys[z, here, :] * (ps[0] - ps[1]), cs[0], cs[1])
                for h in range(HALVES):
                    p, c = ps[h], cs[h]
                    change = carried(cxp[h, z, here, :] * (p - old[h, z + 1, up, :]), c, cc[s, h, z, up, :])
                    change = change + carried(cxp[h, z, down, :] * (p - old[h, z + 1, down, :]), c, cc[s, h, z, down, :])
                    side = jnp.where(edge(h, rows), 0.0, rold[h, z, inner, :])
                    change = change + carried(cyr[h, z, here, :] * (p - side), c, cr[h, z, flat, :])
                    change = change + between if h == 0 else change - between
                    over = cc[s, h, z + 1, here, :] if z < fine - 1 else wrap[h][1]
                    high = carried(cz[h, z + 1, here, :] * (p - old[h, z + 2, here, :] + lift[h, z + 1, here, :]), c, over)
                    change = change + (high - low[h])
                    low[h] = high
                    fresh = c - rl[h, z, flat, :] * change
                    cc[s + 1, h, z, here, :] = fresh
                    if final:
                        continue
                    if row == 0:
                        xs[s + 1, 0, h, z] = fresh[0:W]
                    if row + rows == n:
                        xs[s + 1, 1, h, z] = fresh[rows - W:rows]
                    for j in range(2 * W):
                        at, zj = divmod(lanes + j if j < W else j, fine)
                        if zj == z:
                            k = h * 2 * W + j
                            slab = jnp.where(k_slab == k, pltpu.roll(fresh, (k - at) % lanes, 1), slab)
            if final:
                return
            zs[s + 1, flat, :] = slab
            if row == 0:
                es[s + 1, 0] = slab[0:W]
            if row + rows == n:
                es[s + 1, 1] = slab[rows - W:rows]

        if not final:
            transport(0, 8)
            transport(n - 8, 8)
            start(halo_copies(s + 1, True))
            transport(8, n - 16)
            start(halo_copies(s + 1, False))
            send_totals(s + 1, [own_sum([cc[s + 1, h, z, center, :] for z in range(fine)]) for h in range(HALVES)])
            turn(s + 1)
        else:
            out = pltpu.make_async_copy(old.at[:, pl.ds(1, fine), center, :], p_out, out_sem.at[0])
            out.start()
            transport(0, n)
            last = pltpu.make_async_copy(cc.at[s + 1, :, :, center, :], c_out, out_sem.at[1])
            last.start()
            out.wait()
            last.wait()

    for s in range(STEPS):
        step(s, s == STEPS - 1)


def hand_out(p, c, p_out, c_out, p_cells, c_cells, p_block, c_block, in_sem, out_sem):
    fine, n, lanes = p.shape[1:]
    per = lanes // GROUPS
    parts = [pl.ds(r, PART) for r in range(0, n, PART)]
    fields = ((p, p_cells, p_block, p_out), (c, c_cells, c_block, c_out))
    loads = [[pltpu.make_async_copy(src.at[:, :, part, :], cells.at[:, :, part, :], in_sem.at[a, i])
              for a, (src, cells, _, _) in enumerate(fields)] for i, part in enumerate(parts)]
    stores = [[pltpu.make_async_copy(block.at[:, part, :], dst.at[:, part, :], out_sem.at[a, i])
               for a, (_, _, block, dst) in enumerate(fields)] for i, part in enumerate(parts)]
    for pair in loads:
        for load in pair:
            load.start()
    ln = lax.broadcasted_iota(jnp.int32, (PART, lanes), 1)
    res, grp = (ln + W) % fine, ln // per
    for i, part in enumerate(parts):
        for a, (_, cells, block, _) in enumerate(fields):
            loads[i][a].wait()
            for h in range(HALVES):
                vals = [cells[h, z, part, :] for z in range(fine)]
                moved = []
                for d in range(fine):
                    comb = vals[d]
                    for g in range(1, GROUPS):
                        comb = jnp.where(grp == g, vals[(g + d) % fine], comb)
                    g = jnp.minimum((res - d + fine) % fine, GROUPS - 1)
                    moved.append(jnp.take_along_axis(comb, g * per + (ln + W) // fine, axis=1, mode="promise_in_bounds"))
                for g in range(GROUPS):
                    v = moved[0]
                    for d in range(1, fine):
                        v = jnp.where(res == (g + d) % fine, moved[d], v)
                    block[HALVES * g + h, part, :] = v
            stores[i][a].start()
    for pair in stores:
        for store in pair:
            store.wait()


def on_device(nx, nz, *args):
    ny, n, lanes = args[0].shape
    wide = n + 2 * W
    rows = wide + 2 * LO
    per = lanes // GROUPS
    fine = -(-(lanes + 2 * W) // per)
    copies = 8 + 3 * (nz - 1)

    def vmem(*shape):
        return pltpu.VMEM(shape, jnp.float32)

    padded, plain, own = (HALVES, fine, rows, lanes), (HALVES, fine, wide, lanes), (HALVES, fine, n, lanes)
    slots = (HALVES, fine + 2, rows, lanes)
    scratch = [pltpu.VMEM((ny, n, lanes), a.dtype) for a in args]
    scratch += [vmem(ny, n, lanes)] * 2 + [vmem(FIELDS, ny, 2 * W, lanes)]
    scratch += [vmem(FIELDS - 1, *padded), vmem(STEPS + 1, *padded), vmem(*slots), vmem(*slots)]
    scratch += [vmem(*plain), vmem(*plain), vmem(*own)]
    scratch += [vmem(*plain)] * 10
    scratch += [vmem(*padded), vmem(fine, rows, lanes), vmem(*padded), vmem(HALVES, fine + 1, rows, lanes),
                vmem(HALVES, fine + 1, rows, lanes), vmem(*own), vmem(*plain)]
    scratch += [pltpu.VMEM((4 * lanes, lanes), jnp.bfloat16), vmem(2, W, lanes), vmem(HALVES, wide, lanes),
                vmem(HALVES, n, lanes)]
    scratch += [vmem(STEPS, 2, HALVES, fine, W, lanes)] * 2
    scratch += [vmem(STEPS, n, lanes), vmem(STEPS, 2, n, lanes)]
    scratch += [vmem(STEPS, 2, W, lanes), vmem(STEPS, 2, 2, W, lanes)]
    scratch += [vmem(STEPS, 8, lanes), vmem(STEPS, 3, nz - 1, 8, lanes)]
    scratch += [vmem(2, FIELDS, HALVES, fine, W, lanes)] * 2
    scratch += [vmem(FIELDS, n, lanes), vmem(2, FIELDS, n, lanes), vmem(2, FIELDS, W, lanes), vmem(2, 2, FIELDS, W, lanes)]
    scratch += [pltpu.SemaphoreType.DMA((STEPS, copies))] * 2 + [pltpu.SemaphoreType.DMA((8,))] * 2
    scratch += [pltpu.SemaphoreType.DMA((5,)), pltpu.SemaphoreType.DMA((2,))]
    cells = pl.pallas_call(
        functools.partial(kernel, nx, nz),
        out_shape=[jax.ShapeDtypeStruct(own, jnp.float32)] * 2,
        in_specs=[pl.BlockSpec(memory_space=pltpu.HBM)] * 5,
        out_specs=[pl.BlockSpec(memory_space=pltpu.HBM)] * 2,
        scratch_shapes=scratch,
        compiler_params=pltpu.CompilerParams(
            collective_id=0, has_side_effects=True, vmem_limit_bytes=63 * 1024 * 1024),
    )(*args)
    return tuple(pl.pallas_call(
        hand_out,
        out_shape=[jax.ShapeDtypeStruct((ny, n, lanes), jnp.float32)] * 2,
        in_specs=[pl.BlockSpec(memory_space=pltpu.HBM)] * 2,
        out_specs=[pl.BlockSpec(memory_space=pltpu.HBM)] * 2,
        scratch_shapes=[vmem(*own)] * 2 + [vmem(ny, n, lanes)] * 2 + [pltpu.SemaphoreType.DMA((2, n // PART))] * 2,
        compiler_params=pltpu.CompilerParams(vmem_limit_bytes=63 * 1024 * 1024),
    )(*cells))


def solution(mesh):
    placed = P(None, "gx", "gz")
    return jax.shard_map(
        functools.partial(on_device, mesh.shape["gx"], mesh.shape["gz"]),
        mesh=mesh,
        in_specs=(placed,) * 5,
        out_specs=(placed, placed),
        check_vma=False,
    )
```

```python
import functools

import jax
import jax.numpy as jnp
from jax import lax
from jax.experimental import pallas as pl
from jax.experimental.pallas import tpu as pltpu
from jax.sharding import PartitionSpec as P

STEPS = 4
SWEEPS = 3
W = SWEEPS + 1
SOLUTE_RATE = 0.5
MESH = pl.DeviceIdType.MESH
GROUPS = 8
HALVES = 2
FIELDS = 4
LO = 12
PART = 16


def kernel(nx, nz, *refs):
    it = iter(refs)
    hbm = [next(it) for _ in range(5)]
    p_out, c_out = [next(it) for _ in range(2)]
    t_in, c_in, f_in, k_in, m_in = staged = [next(it) for _ in range(5)]
    o_pm, o_liq, strip = [next(it) for _ in range(3)]
    stat, cc, cr = [next(it) for _ in range(3)]
    press = [next(it) for _ in range(W)]
    turned = [next(it) for _ in range(W)]
    axp, axm, ays, ayr, azp, azm, srcn, bb, gr, rh = [next(it) for _ in range(10)]
    cxp, cys, cyr, cz, lift, rl, tt = [next(it) for _ in range(7)]
    wts, hz, off, sm, ab, tt0 = [next(it) for _ in range(6)]
    xs, xr, zs, zr, es, er, ts, td, tr = [next(it) for _ in range(9)]
    sxs, sxr, szs, szr, ses, ser = [next(it) for _ in range(6)]
    send_sem, recv_sem, st_send, st_recv, in_sem, out_sem = [next(it) for _ in range(6)]

    ny, n, lanes = t_in.shape
    wide = n + 2 * W
    per = lanes // GROUPS
    fine = stat.shape[2]
    mid = LO + W
    blocks = n // 8
    gravity = 4.0 / (nz * lanes)
    half = 0.5 * gravity
    ix, iz = lax.axis_index("gx"), lax.axis_index("gz")
    f32, bf16 = jnp.float32, jnp.bfloat16
    PERM, TEMP, LIQ, CONC = range(FIELDS)

    def inside(dx, dz):
        return (ix + dx >= 0) & (ix + dx < nx) & (iz + dz >= 0) & (iz + dz < nz)

    partners = [(dx, dz) for dz in range(-1, nz) for dx in (-1, 0, 1) if (dx, dz) != (0, 0)]

    def remote(src, dst, send, recv, dx, dz):
        return dx, dz, pltpu.make_async_remote_copy(
            src_ref=src, dst_ref=dst, send_sem=send, recv_sem=recv,
            device_id={"gx": ix + dx, "gz": iz + dz}, device_id_type=MESH)

    near = [(dx, dz) for dx, dz in partners if dz <= 1]

    def halo_copies(s, along_x):
        out = []
        for m, (dx, dz) in enumerate(near):
            a, b = (1, 0) if dx > 0 else (0, 1)
            side = 0 if dz > 0 else 1
            if dz == 0:
                src, dst = xs.at[s, a], xr.at[s, b]
            elif dx == 0:
                src, dst = zs.at[s], zr.at[s, side]
            else:
                src, dst = es.at[s, a], er.at[s, b, side]
            if (dx != 0) == along_x:
                out.append(remote(src, dst, send_sem.at[m], recv_sem.at[s, m], dx, dz))
        return sorted(out, key=lambda item: item[1] != 0)

    def total_copies(s, along_x):
        below = [(dx, dz) for dx, dz in partners if dz > 0]
        return [remote((td if along_x else ts).at[s], tr.at[s, 1 - dx, dz - 1],
                       send_sem.at[len(near) + m], recv_sem.at[s, len(near) + m], dx, dz)
                for m, (dx, dz) in enumerate(below) if (dx != 0) == along_x]

    def static_copies(along_x):
        out = []
        for m, (dx, dz) in enumerate(near):
            a, b = (1, 0) if dx > 0 else (0, 1)
            side = 0 if dz > 0 else 1
            if dz == 0:
                src, dst = sxs.at[a], sxr.at[b]
            elif dx == 0:
                src, dst = szs, szr.at[side]
            else:
                src, dst = ses.at[a], ser.at[b, side]
            if (dx != 0) == along_x:
                out.append(remote(src, dst, st_send.at[m], st_recv.at[m], dx, dz))
        return sorted(out, key=lambda item: item[1] != 0)

    def start(copies):
        for dx, dz, c in copies:
            pl.when(inside(dx, dz))(c.start)

    def arrive(copies):
        for dx, dz, c in copies:
            pl.when(inside(-dx, -dz))(c.wait_recv)

    def sent(copies):
        for dx, dz, c in copies:
            pl.when(inside(dx, dz))(c.wait_send)

    loads = [pltpu.make_async_copy(a, b, in_sem.at[i]) for i, (a, b) in enumerate(zip(hbm, staged))]
    for load in loads:
        load.start()

    for ref in (xr, zr, er, tr, sxr, szr, ser):
        ref[...] = jnp.zeros_like(ref)
    barrier = pltpu.get_barrier_semaphore()
    count = 0
    for dx, dz in partners:
        @pl.when(inside(-dx, -dz))
        def _(dx=dx, dz=dz):
            pl.semaphore_signal(barrier, inc=1, device_id={"gx": ix - dx, "gz": iz - dz}, device_id_type=MESH)
        count = count + inside(dx, dz).astype(jnp.int32)

    def lane(rows):
        return lax.broadcasted_iota(jnp.int32, (rows, lanes), 1)

    def split(value):
        high = value.astype(bf16)
        low = (value - high.astype(f32)).astype(bf16)
        return jnp.concatenate([high, low], axis=1)

    r2 = lax.broadcasted_iota(jnp.int32, (2 * lanes, lanes), 0) % lanes
    c2 = lax.broadcasted_iota(jnp.int32, (2 * lanes, lanes), 1)
    same = (r2 // per) == (c2 // per)
    wts[0:2 * lanes] = jnp.where(same, jnp.where(r2 < c2, 1.0, 0.0), 0.0).astype(bf16)
    wts[2 * lanes:4 * lanes] = jnp.where(same, 1.0, 0.0).astype(bf16)

    zrows = jnp.zeros((8, lanes), f32)
    for h in range(HALVES):
        for z in range(fine):
            for r in (LO - 4, LO + wide - 4):
                stat[PERM, h, z, r:r + 8] = zrows

    for load in loads:
        load.wait()
    center = pl.ds(mid, n)
    window = pl.ds(LO, wide)
    top, bottom = pl.ds(LO, W), pl.ds(mid + n, W)

    ln = lane(n)
    packed = [jnp.zeros((n, lanes), f32)] * FIELDS
    for y in range(ny):
        mark, t, c = m_in[y], t_in[y], c_in[y]
        liq = jnp.where(mark == 1, 1.0, jnp.where(mark == 2, 0.0, f_in[y]))
        solid = 1.0 - liq
        pm = k_in[y] * (liq * liq * liq / (solid * solid + 0.25) + 0.02)
        o_pm[y] = pm
        o_liq[y] = liq
        for f, v in enumerate((pm, t, liq, c)):
            strip[f, y, 0:W] = v[0:W]
            strip[f, y, W:2 * W] = v[n - W:n]
            packed[f] = jnp.where(ln // (2 * W) == y, pltpu.roll(v, (y * 2 * W + W) % lanes, 1), packed[f])
    for f in range(FIELDS):
        szs[f] = packed[f]
        ses[0, f] = packed[f][0:W]
        ses[1, f] = packed[f][n - W:n]

    def spread(get, put, rows):
        lw = lane(rows)
        res, grp, zc = (lw + W) % fine, lw // per, lw % per
        for h in range(HALVES):
            vals = [get(HALVES * g + h) for g in range(GROUPS)]
            moved = []
            for d in range(fine):
                comb = vals[0]
                for g in range(1, GROUPS):
                    comb = jnp.where(res == (g + d) % fine, vals[g], comb)
                z = fine * zc + (grp + d) % fine - W
                moved.append(jnp.take_along_axis(comb, jnp.clip(z, 0, lanes - 1), axis=1, mode="promise_in_bounds"))
            for z in range(fine):
                v = moved[z]
                for g in range(1, GROUPS):
                    v = jnp.where(grp == g, moved[(z - g) % fine], v)
                zw = fine * zc + z
                put(h, z, jnp.where((zw >= W) & (zw < W + lanes), v, 0.0))

    for f in range(FIELDS):
        def put(h, z, v, f=f):
            sxs[0, f, h, z] = v[0:W]
            sxs[1, f, h, z] = v[W:2 * W]
        spread(lambda y, f=f: strip[f, y], put, 2 * W)
    pl.semaphore_wait(barrier, count)
    start(static_copies(True))
    start(static_copies(False))

    def cells(f):
        return cc.at[0] if f == CONC else stat.at[f]

    for f, ref in ((CONC, c_in), (TEMP, t_in), (PERM, o_pm), (LIQ, o_liq)):
        for r in range(0, n, 16):
            def put(h, z, v, f=f, r=r):
                cells(f)[h, z, mid + r:mid + r + 16, :] = v
            spread(lambda y, ref=ref, r=r: ref[y, r:r + 16], put, 16)

    def own_sum(values, rows):
        zc = lane(rows) % per
        out = jnp.zeros((rows, lanes), f32)
        for first in sorted({0, W % fine, (W + lanes) % fine}):
            last = min([e for e in (W % fine, (W + lanes) % fine, fine) if e > first])
            part = values[first]
            for z in range(first + 1, last):
                part = part + values[z]
            zw = fine * zc + first
            out = out + jnp.where((zw >= W) & (zw < W + lanes), part, 0.0)
        return out

    def send_totals(s, along_x):
        parts = [(0, 8), (n - 8, 8)] if along_x else [(0, n)]
        sums = []
        for h in range(HALVES):
            for row, rows in parts:
                conc = own_sum([cc[s, h, z, pl.ds(mid + row, rows), :] for z in range(fine)], rows)
                sums.append(split(tt0[h, row:row + rows] + 0.2 * conc))
        tot = jnp.dot(jnp.concatenate(sums, axis=0), wts[2 * lanes:4 * lanes], preferred_element_type=f32)
        slot = lane(8) % per
        out = jnp.zeros((8, lanes), f32)
        places = [h * blocks + j for h in range(HALVES) for row, rows in parts for j in range(row // 8, (row + rows) // 8)]
        for i, place in enumerate(places):
            out = jnp.where(slot == place, tot[8 * i:8 * i + 8], out)
        (td if along_x else ts)[s] = out
        start(total_copies(s, along_x))

    def edge(h, rows):
        return lane(rows) < per if h == 0 else lane(rows) >= lanes - per

    shift = (per, lanes - per)

    def turn(s):
        for h in range(HALVES):
            for z in range(fine):
                cr[h, z] = jnp.where(edge(h, n), 0.0, pltpu.roll(cc[s, 1 - h, z, center, :], shift[h], 1))

    for h in range(HALVES):
        tt0[h] = own_sum([1.0 - 0.3 * stat[TEMP, h, z, center, :] for z in range(fine)], n)
    send_totals(0, True)
    send_totals(0, False)
    turn(0)

    def insert(dst, packed, row, rows):
        zc, at_rows = lane(rows) % per, pl.ds(LO + row, rows)
        for h in range(HALVES):
            for k in range(2 * W):
                at, z = divmod(k if k < W else lanes + k, fine)
                moved = pltpu.roll(packed, (at - h * 2 * W - k) % lanes, 1)
                dst[h, z, at_rows, :] = jnp.where(zc == at, moved, dst[h, z, at_rows, :])

    def insert_strips(dst, strips, corners):
        for h in range(HALVES):
            for z in range(fine):
                dst[h, z, top, :] = strips(0, h, z)
                dst[h, z, bottom, :] = strips(1, h, z)
        for b in range(2):
            hz[b] = jnp.where(k_e < W, corners(b, 0), corners(b, 1))
            insert(dst, hz[b], b * (n + W), W)

    k_n, k_e = lane(n) % (2 * W), lane(W) % (2 * W)

    def coefficients(row, rows):
        here, up, down, flat = pl.ds(LO + row, rows), pl.ds(LO + row + 1, rows), pl.ds(LO + row - 1, rows), pl.ds(row, rows)
        beside = [edge(h, rows) for h in range(HALVES)]
        for h in range(HALVES):
            for z in range(fine):
                pm = stat[PERM, h, z, here, :]
                over = stat[PERM, h, z + 1, here, :] if z < fine - 1 else pltpu.roll(stat[PERM, h, 0, here, :], lanes - 1, 1)
                under = stat[PERM, h, z - 1, here, :] if z > 0 else pltpu.roll(stat[PERM, h, fine - 1, here, :], 1, 1)
                cross = jnp.where(beside[h], 0.0, pltpu.roll(stat[PERM, 1 - h, z, here, :], shift[h], 1))
                c = [0.5 * (pm + other) for other in (
                    stat[PERM, h, z, up, :], stat[PERM, h, z, down, :], stat[PERM, 1 - h, z, here, :], cross, over, under)]
                total = c[0] + c[1] + c[2] + c[3] + c[4] + c[5]
                real = pm > 0.0
                inv = jnp.where(real, 1.0 / jnp.where(real, total, 1.0), 0.0)
                cxp[h, z, here, :] = c[0]
                if h == 0:
                    cys[z, here, :] = c[2]
                cyr[h, z, here, :] = c[3]
                cz[h, z + 1, here, :] = c[4]
                if z == 0:
                    cz[h, 0, here, :] = c[5]
                axp[h, z, flat] = c[0] * inv
                axm[h, z, flat] = c[1] * inv
                ays[h, z, flat] = c[2] * inv
                ayr[h, z, flat] = jnp.where(beside[h], 0.0, c[3] * inv)
                azp[h, z, flat] = c[4] * inv
                azm[h, z, flat] = c[5] * inv
                liq, t = stat[LIQ, h, z, here, :], stat[TEMP, h, z, here, :]
                srcn[h, z, flat] = 2.0 * liq * (1.0 - liq) * t * inv
                tt[h, z, flat] = jnp.where(real, 1.0 - 0.3 * t, 0.0)
                gr[h, z, flat] = jnp.where(real, gravity, 0.0)

    def keep(sweep, h, z, row, rows, v):
        p, r = press[sweep], turned[sweep]
        at_rows = pl.ds(LO + row, rows)
        p[h, z + 1, at_rows, :] = v
        r[1 - h, z, pl.ds(row, rows), :] = pltpu.roll(v, shift[1 - h], 1)
        if z == 0:
            p[h, fine + 1, at_rows, :] = pltpu.roll(v, lanes - 1, 1)
        if z == fine - 1:
            p[h, 0, at_rows, :] = pltpu.roll(v, 1, 1)

    order = [0, fine - 1] + list(range(1, fine - 1))

    def carried(flow, own, other):
        return flow * jnp.where(flow > 0.0, own, other)

    def forces(s, row, rows):
        here, flat = pl.ds(LO + row, rows), pl.ds(row, rows)
        first_lane = lane(rows) % per == 0
        for h in range(HALVES):
            for z in range(fine):
                rh[h, z, flat, :] = tt[h, z, flat, :] + 0.2 * cc[s, h, z, here, :]
            before = rh[h, 0, flat, :]
            for z in range(1, W):
                before = before + rh[h, z, flat, :]
            run = jnp.where(first_lane, -before, 0.0)
            lo = half * (pltpu.roll(rh[h, fine - 1, flat, :], 1, 1) + rh[h, 0, flat, :])
            lift[h, 0, here, :] = lo
            for z in range(fine):
                rho = rh[h, z, flat, :]
                press[0][h, z + 1, here, :] = run + 0.5 * rho
                run = run + rho
                other = rh[h, z + 1, flat, :] if z < fine - 1 else pltpu.roll(rh[h, 0, flat, :], lanes - 1, 1)
                hi = half * (rho + other)
                lift[h, z + 1, here, :] = hi
                bb[h, z, flat, :] = srcn[h, z, flat, :] - azp[h, z, flat, :] * hi + azm[h, z, flat, :] * lo
                lo = hi
            sm[h, flat, :] = run

    def above(parts):
        rows_in = [(h, pl.ds(row, rows)) for h in range(HALVES) for row, rows in parts]
        both = jnp.concatenate([jnp.concatenate([split(sm[h, at, :]), split(off[h, at, :])], axis=1) for h, at in rows_in], axis=0)
        base = jnp.dot(both, wts[...], preferred_element_type=f32)
        done = 0
        for h in range(HALVES):
            for row, rows in parts:
                ab[h, pl.ds(row, rows), :] = base[done:done + rows]
                done += rows

    def heads(row, rows):
        here, flat = pl.ds(LO + row, rows), pl.ds(row, rows)
        for z in order:
            for h in range(HALVES):
                keep(0, h, z, row, rows, gr[h, z, flat, :] * (press[0][h, z + 1, here, :] + ab[h, flat, :]))

    def relax(sweep, row, rows):
        old, rold = press[sweep], turned[sweep]
        here, flat = pl.ds(LO + row, rows), pl.ds(row, rows)
        up, down = pl.ds(LO + row + 1, rows), pl.ds(LO + row - 1, rows)
        for z in order:
            for h in range(HALVES):
                v = bb[h, z, flat, :] + axp[h, z, flat, :] * old[h, z + 1, up, :] + axm[h, z, flat, :] * old[h, z + 1, down, :]
                v = v + (ays[h, z, flat, :] * old[1 - h, z + 1, here, :] + ayr[h, z, flat, :] * rold[h, z, flat, :])
                v = v + (azp[h, z, flat, :] * old[h, z + 2, here, :] + azm[h, z, flat, :] * old[h, z, here, :])
                keep(sweep + 1, h, z, row, rows, v)

    def ends(row):
        return [(row, 8), (wide - 8 - row, 8)]

    def received(s, side):
        total = tr[s, side, 0]
        for d in range(1, nz - 1):
            total = total + tr[s, side, d]
        return total

    old, rold = press[SWEEPS], turned[SWEEPS]

    def step(s, final):
        lead = W if s > 0 else 8
        def transport(row, rows):
            here, up, down = pl.ds(mid + row, rows), pl.ds(mid + row + 1, rows), pl.ds(mid + row - 1, rows)
            flat, inner = pl.ds(row, rows), pl.ds(W + row, rows)
            slab = jnp.zeros((rows, lanes), f32)
            k_slab = lane(rows) % per
            wrap = [(pltpu.roll(cc[s, h, fine - 1, here, :], 1, 1), pltpu.roll(cc[s, h, 0, here, :], lanes - 1, 1))
                    for h in range(HALVES)]
            low = [carried(cz[h, 0, here, :] * (old[h, 0, here, :] - old[h, 1, here, :] + lift[h, 0, here, :]),
                           wrap[h][0], cc[s, h, 0, here, :]) for h in range(HALVES)]
            for z in range(fine):
                ps = [old[h, z + 1, here, :] for h in range(HALVES)]
                cs = [cc[s, h, z, here, :] for h in range(HALVES)]
                between = carried(cys[z, here, :] * (ps[0] - ps[1]), cs[0], cs[1])
                for h in range(HALVES):
                    p, c = ps[h], cs[h]
                    change = carried(cxp[h, z, here, :] * (p - old[h, z + 1, up, :]), c, cc[s, h, z, up, :])
                    change = change + carried(cxp[h, z, down, :] * (p - old[h, z + 1, down, :]), c, cc[s, h, z, down, :])
                    side = jnp.where(edge(h, rows), 0.0, rold[h, z, inner, :])
                    change = change + carried(cyr[h, z, here, :] * (p - side), c, cr[h, z, flat, :])
                    change = change + between if h == 0 else change - between
                    over = cc[s, h, z + 1, here, :] if z < fine - 1 else wrap[h][1]
                    high = carried(cz[h, z + 1, here, :] * (p - old[h, z + 2, here, :] + lift[h, z + 1, here, :]), c, over)
                    change = change + (high - low[h])
                    low[h] = high
                    fresh = c - rl[h, z, flat, :] * change
                    cc[s + 1, h, z, here, :] = fresh
                    if final:
                        continue
                    if row == 0:
                        xs[s + 1, 0, h, z] = fresh[0:W]
                    if row + rows == n:
                        xs[s + 1, 1, h, z] = fresh[rows - W:rows]
                    for j in range(2 * W):
                        at, zj = divmod(lanes + j if j < W else j, fine)
                        if zj == z:
                            k = h * 2 * W + j
                            slab = jnp.where(k_slab == k, pltpu.roll(fresh, (k - at) % lanes, 1), slab)
            if final:
                return
            zs[s + 1, flat, :] = slab
            if row == 0:
                es[s + 1, 0] = slab[0:W]
            if row + rows == n:
                es[s + 1, 1] = slab[rows - W:rows]

        slot = lane(8) % per
        if s > 0:
            sent(halo_copies(s, True))
            sent(halo_copies(s, False))
            sent(total_copies(s, True))
            sent(total_copies(s, False))
            arrive(halo_copies(s, False))
            insert(cc.at[s], jnp.where(k_n < W, zr[s, 0], zr[s, 1]), W, n)
        else:
            arrive(static_copies(False))
            for f in range(FIELDS):
                insert(cells(f), jnp.where(k_n < W, szr[0, f], szr[1, f]), W, n)
            zc_n = lane(n) % per
            for h in range(HALVES):
                for z in range(fine):
                    zw = fine * zc_n + z
                    rl[h, z] = jnp.where((zw >= W) & (zw < W + lanes),
                                         SOLUTE_RATE / (stat[LIQ, h, z, center, :] + 0.1), 0.0)
            coefficients(lead, wide - 2 * lead)
            sent(static_copies(False))
            sent(total_copies(0, True))
            sent(total_copies(0, False))
        inner = (lead, wide - 2 * lead)
        forces(s, *inner)
        arrive(total_copies(s, False))
        below = received(s, 1)
        for h in range(HALVES):
            for j in range(blocks):
                off[h, W + 8 * j:W + 8 * j + 8] = jnp.where(slot == h * blocks + j, below, 0.0)
        above([inner])
        heads(*inner)
        for sweep in range(SWEEPS):
            relax(sweep, lead + 1 + sweep, wide - 2 * (lead + 1 + sweep))
        transport(lead, n - 2 * lead)

        if s > 0:
            arrive(halo_copies(s, True))
            insert_strips(cc.at[s], lambda b, h, z: xr[s, b, h, z], lambda b, side: er[s, b, side])
        else:
            arrive(static_copies(True))
            for f in range(FIELDS):
                insert_strips(cells(f), lambda b, h, z, f=f: sxr[b, f, h, z], lambda b, side, f=f: ser[b, side, f])
            for end in ends(0):
                coefficients(*end)
            sent(static_copies(True))
        for end in ends(0):
            forces(s, *end)
        arrive(total_copies(s, True))
        left, right = received(s, 0), received(s, 2)
        for h in range(HALVES):
            off[h, 0:W] = jnp.where(slot == h * blocks + blocks - 1, left, 0.0)[8 - W:8]
            off[h, W + n:wide] = jnp.where(slot == h * blocks, right, 0.0)[0:W]
        above(ends(0))
        for end in ends(0):
            heads(*end)
        for sweep in range(SWEEPS):
            for end in ends(sweep + 1):
                relax(sweep, *end)
        if not final:
            transport(0, 8)
            transport(n - 8, 8)
            start(halo_copies(s + 1, True))
            send_totals(s + 1, True)
            start(halo_copies(s + 1, False))
            send_totals(s + 1, False)
            turn(s + 1)
        else:
            out = pltpu.make_async_copy(old.at[:, pl.ds(1, fine), center, :], p_out, out_sem.at[0])
            out.start()
            transport(0, 8)
            transport(n - 8, 8)
            last = pltpu.make_async_copy(cc.at[s + 1, :, :, center, :], c_out, out_sem.at[1])
            last.start()
            out.wait()
            last.wait()

    for s in range(STEPS):
        step(s, s == STEPS - 1)


def hand_out(p, c, p_out, c_out, p_cells, c_cells, p_block, c_block, in_sem, out_sem):
    fine, n, lanes = p.shape[1:]
    per = lanes // GROUPS
    parts = [pl.ds(r, PART) for r in range(0, n, PART)]
    fields = ((p, p_cells, p_block, p_out), (c, c_cells, c_block, c_out))
    loads = [[pltpu.make_async_copy(src.at[:, :, part, :], cells.at[:, :, part, :], in_sem.at[a, i])
              for a, (src, cells, _, _) in enumerate(fields)] for i, part in enumerate(parts)]
    stores = [[pltpu.make_async_copy(block.at[:, part, :], dst.at[:, part, :], out_sem.at[a, i])
               for a, (_, _, block, dst) in enumerate(fields)] for i, part in enumerate(parts)]
    for pair in loads:
        for load in pair:
            load.start()
    ln = lax.broadcasted_iota(jnp.int32, (PART, lanes), 1)
    res, grp = (ln + W) % fine, ln // per
    for i, part in enumerate(parts):
        for a, (_, cells, block, _) in enumerate(fields):
            loads[i][a].wait()
            for h in range(HALVES):
                vals = [cells[h, z, part, :] for z in range(fine)]
                moved = []
                for d in range(fine):
                    comb = vals[d]
                    for g in range(1, GROUPS):
                        comb = jnp.where(grp == g, vals[(g + d) % fine], comb)
                    g = jnp.minimum((res - d + fine) % fine, GROUPS - 1)
                    moved.append(jnp.take_along_axis(comb, g * per + (ln + W) // fine, axis=1, mode="promise_in_bounds"))
                for g in range(GROUPS):
                    v = moved[0]
                    for d in range(1, fine):
                        v = jnp.where(res == (g + d) % fine, moved[d], v)
                    block[HALVES * g + h, part, :] = v
            stores[i][a].start()
    for pair in stores:
        for store in pair:
            store.wait()


def on_device(nx, nz, *args):
    ny, n, lanes = args[0].shape
    wide = n + 2 * W
    rows = wide + 2 * LO
    per = lanes // GROUPS
    fine = -(-(lanes + 2 * W) // per)
    copies = 8 + 3 * (nz - 1)

    def vmem(*shape):
        return pltpu.VMEM(shape, jnp.float32)

    padded, plain, own = (HALVES, fine, rows, lanes), (HALVES, fine, wide, lanes), (HALVES, fine, n, lanes)
    slots = (HALVES, fine + 2, rows, lanes)
    scratch = [pltpu.VMEM((ny, n, lanes), a.dtype) for a in args]
    scratch += [vmem(ny, n, lanes)] * 2 + [vmem(FIELDS, ny, 2 * W, lanes)]
    scratch += [vmem(FIELDS - 1, *padded), vmem(STEPS + 1, *padded), vmem(*own)]
    scratch += [vmem(*slots)] * W + [vmem(*plain)] * W
    scratch += [vmem(*plain)] * 10
    scratch += [vmem(*padded), vmem(fine, rows, lanes), vmem(*padded), vmem(HALVES, fine + 1, rows, lanes),
                vmem(HALVES, fine + 1, rows, lanes), vmem(*own), vmem(*plain)]
    scratch += [pltpu.VMEM((4 * lanes, lanes), jnp.bfloat16), vmem(2, W, lanes)] + [vmem(HALVES, wide, lanes)] * 3
    scratch += [vmem(HALVES, n, lanes)]
    scratch += [vmem(STEPS, 2, HALVES, fine, W, lanes)] * 2
    scratch += [vmem(STEPS, n, lanes), vmem(STEPS, 2, n, lanes)]
    scratch += [vmem(STEPS, 2, W, lanes), vmem(STEPS, 2, 2, W, lanes)]
    scratch += [vmem(STEPS, 8, lanes)] * 2 + [vmem(STEPS, 3, nz - 1, 8, lanes)]
    scratch += [vmem(2, FIELDS, HALVES, fine, W, lanes)] * 2
    scratch += [vmem(FIELDS, n, lanes), vmem(2, FIELDS, n, lanes), vmem(2, FIELDS, W, lanes), vmem(2, 2, FIELDS, W, lanes)]
    scratch += [pltpu.SemaphoreType.DMA((copies,)), pltpu.SemaphoreType.DMA((STEPS, copies))] + [pltpu.SemaphoreType.DMA((8,))] * 2
    scratch += [pltpu.SemaphoreType.DMA((5,)), pltpu.SemaphoreType.DMA((2,))]
    cells = pl.pallas_call(
        functools.partial(kernel, nx, nz),
        out_shape=[jax.ShapeDtypeStruct(own, jnp.float32)] * 2,
        in_specs=[pl.BlockSpec(memory_space=pltpu.HBM)] * 5,
        out_specs=[pl.BlockSpec(memory_space=pltpu.HBM)] * 2,
        scratch_shapes=scratch,
        compiler_params=pltpu.CompilerParams(
            collective_id=0, has_side_effects=True, vmem_limit_bytes=63 * 1024 * 1024),
    )(*args)
    return tuple(pl.pallas_call(
        hand_out,
        out_shape=[jax.ShapeDtypeStruct((ny, n, lanes), jnp.float32)] * 2,
        in_specs=[pl.BlockSpec(memory_space=pltpu.HBM)] * 2,
        out_specs=[pl.BlockSpec(memory_space=pltpu.HBM)] * 2,
        scratch_shapes=[vmem(*own)] * 2 + [vmem(ny, n, lanes)] * 2 + [pltpu.SemaphoreType.DMA((2, n // PART))] * 2,
        compiler_params=pltpu.CompilerParams(vmem_limit_bytes=63 * 1024 * 1024),
    )(*cells))


def solution(mesh):
    placed = P(None, "gx", "gz")
    return jax.shard_map(
        functools.partial(on_device, mesh.shape["gx"], mesh.shape["gz"]),
        mesh=mesh,
        in_specs=(placed,) * 5,
        out_specs=(placed, placed),
        check_vma=False,
    )
```

```python
import functools

import jax
import jax.numpy as jnp
from jax import lax
from jax.experimental import pallas as pl
from jax.experimental.pallas import tpu as pltpu
from jax.sharding import PartitionSpec as P

STEPS = 4
SWEEPS = 3
W = SWEEPS + 1
SOLUTE_RATE = 0.5
MESH = pl.DeviceIdType.MESH
GROUPS = 8
HALVES = 2
FIELDS = 4
LO = 12
PART = 16


def kernel(nx, nz, *refs):
    it = iter(refs)
    hbm = [next(it) for _ in range(5)]
    p_out, c_out = [next(it) for _ in range(2)]
    t_in, c_in, f_in, k_in, m_in = staged = [next(it) for _ in range(5)]
    o_pm, o_liq, strip = [next(it) for _ in range(3)]
    stat, cc, cr = [next(it) for _ in range(3)]
    press = [next(it) for _ in range(W)]
    turned = [next(it) for _ in range(W)]
    axp, axm, ays, ayr, azp, azm, srcn, bb, gr, rh = [next(it) for _ in range(10)]
    cxp, cys, cyr, cz, lift, rl, tt = [next(it) for _ in range(7)]
    wts, hz, off, sm, ab, tt0 = [next(it) for _ in range(6)]
    xs, xr, zs, zr, es, er, ts, td, tr = [next(it) for _ in range(9)]
    sxs, sxr, szs, szr, ses, ser = [next(it) for _ in range(6)]
    send_sem, recv_sem, st_send, st_recv, in_sem, out_sem = [next(it) for _ in range(6)]

    ny, n, lanes = t_in.shape
    wide = n + 2 * W
    per = lanes // GROUPS
    fine = stat.shape[2]
    mid = LO + W
    blocks = n // 8
    gravity = 4.0 / (nz * lanes)
    half = 0.5 * gravity
    ix, iz = lax.axis_index("gx"), lax.axis_index("gz")
    f32, bf16 = jnp.float32, jnp.bfloat16
    PERM, TEMP, LIQ, CONC = range(FIELDS)

    def inside(dx, dz):
        return (ix + dx >= 0) & (ix + dx < nx) & (iz + dz >= 0) & (iz + dz < nz)

    partners = [(dx, dz) for dz in range(-1, nz) for dx in (-1, 0, 1) if (dx, dz) != (0, 0)]

    def remote(src, dst, send, recv, dx, dz):
        return dx, dz, pltpu.make_async_remote_copy(
            src_ref=src, dst_ref=dst, send_sem=send, recv_sem=recv,
            device_id={"gx": ix + dx, "gz": iz + dz}, device_id_type=MESH)

    near = [(dx, dz) for dx, dz in partners if dz <= 1]

    def halo_copies(s, along_x):
        out = []
        for m, (dx, dz) in enumerate(near):
            a, b = (1, 0) if dx > 0 else (0, 1)
            side = 0 if dz > 0 else 1
            if dz == 0:
                src, dst = xs.at[s, a], xr.at[s, b]
            elif dx == 0:
                src, dst = zs.at[s], zr.at[s, side]
            else:
                src, dst = es.at[s, a], er.at[s, b, side]
            if (dx != 0) == along_x:
                out.append(remote(src, dst, send_sem.at[m], recv_sem.at[s, m], dx, dz))
        return sorted(out, key=lambda item: item[1] != 0)

    def total_copies(s, along_x):
        below = [(dx, dz) for dx, dz in partners if dz > 0]
        return [remote((td if along_x else ts).at[s], tr.at[s, 1 - dx, dz - 1],
                       send_sem.at[len(near) + m], recv_sem.at[s, len(near) + m], dx, dz)
                for m, (dx, dz) in enumerate(below) if (dx != 0) == along_x]

    def static_copies(dz_only):
        out = []
        for m, (dx, dz) in enumerate(near):
            a, b = (1, 0) if dx > 0 else (0, 1)
            side = 0 if dz > 0 else 1
            if dx == 0:
                src, dst = szs, szr.at[side]
            elif dz != 0:
                src, dst = ses.at[a], ser.at[b, side]
            else:
                continue
            if (dx == 0) == dz_only:
                out.append(remote(src, dst, st_send.at[m], st_recv.at[m], dx, dz))
        return out

    def static_strips(fields, base):
        return [remote(sxs.at[a, fields], sxr.at[1 - a, fields], st_send.at[base + a], st_recv.at[base + a], dx, 0)
                for a, dx in ((1, 1), (0, -1))]

    still, moving = pl.ds(0, FIELDS - 1), pl.ds(FIELDS - 1, 1)

    def start(copies):
        for dx, dz, c in copies:
            pl.when(inside(dx, dz))(c.start)

    def arrive(copies):
        for dx, dz, c in copies:
            pl.when(inside(-dx, -dz))(c.wait_recv)

    def sent(copies):
        for dx, dz, c in copies:
            pl.when(inside(dx, dz))(c.wait_send)

    loads = [pltpu.make_async_copy(a, b, in_sem.at[i]) for i, (a, b) in enumerate(zip(hbm, staged))]
    for load in loads:
        load.start()

    for ref in (xr, zr, er, tr, sxr, szr, ser):
        ref[...] = jnp.zeros_like(ref)
    barrier = pltpu.get_barrier_semaphore()
    count = 0
    for dx, dz in partners:
        @pl.when(inside(-dx, -dz))
        def _(dx=dx, dz=dz):
            pl.semaphore_signal(barrier, inc=1, device_id={"gx": ix - dx, "gz": iz - dz}, device_id_type=MESH)
        count = count + inside(dx, dz).astype(jnp.int32)

    def lane(rows):
        return lax.broadcasted_iota(jnp.int32, (rows, lanes), 1)

    def split(value):
        high = value.astype(bf16)
        low = (value - high.astype(f32)).astype(bf16)
        return jnp.concatenate([high, low], axis=1)

    r2 = lax.broadcasted_iota(jnp.int32, (2 * lanes, lanes), 0) % lanes
    c2 = lax.broadcasted_iota(jnp.int32, (2 * lanes, lanes), 1)
    same = (r2 // per) == (c2 // per)
    wts[0:2 * lanes] = jnp.where(same, jnp.where(r2 < c2, 1.0, 0.0), 0.0).astype(bf16)
    wts[2 * lanes:4 * lanes] = jnp.where(same, 1.0, 0.0).astype(bf16)

    zrows = jnp.zeros((8, lanes), f32)
    for h in range(HALVES):
        for z in range(fine):
            for r in (LO - 4, LO + wide - 4):
                stat[PERM, h, z, r:r + 8] = zrows

    for load in loads:
        load.wait()
    center = pl.ds(mid, n)
    window = pl.ds(LO, wide)
    top, bottom = pl.ds(LO, W), pl.ds(mid + n, W)

    ln = lane(n)
    packed = [jnp.zeros((n, lanes), f32)] * FIELDS
    for y in range(ny):
        mark, t, c = m_in[y], t_in[y], c_in[y]
        liq = jnp.where(mark == 1, 1.0, jnp.where(mark == 2, 0.0, f_in[y]))
        solid = 1.0 - liq
        pm = k_in[y] * (liq * liq * liq / (solid * solid + 0.25) + 0.02)
        o_pm[y] = pm
        o_liq[y] = liq
        for f, v in enumerate((pm, t, liq, c)):
            strip[f, y, 0:W] = v[0:W]
            strip[f, y, W:2 * W] = v[n - W:n]
            packed[f] = jnp.where(ln // (2 * W) == y, pltpu.roll(v, (y * 2 * W + W) % lanes, 1), packed[f])
    for f in range(FIELDS):
        szs[f] = packed[f]
        ses[0, f] = packed[f][0:W]
        ses[1, f] = packed[f][n - W:n]

    def spread(get, put, rows):
        lw = lane(rows)
        res, grp, zc = (lw + W) % fine, lw // per, lw % per
        for h in range(HALVES):
            vals = [get(HALVES * g + h) for g in range(GROUPS)]
            moved = []
            for d in range(fine):
                comb = vals[0]
                for g in range(1, GROUPS):
                    comb = jnp.where(res == (g + d) % fine, vals[g], comb)
                z = fine * zc + (grp + d) % fine - W
                moved.append(jnp.take_along_axis(comb, jnp.clip(z, 0, lanes - 1), axis=1, mode="promise_in_bounds"))
            for z in range(fine):
                v = moved[z]
                for g in range(1, GROUPS):
                    v = jnp.where(grp == g, moved[(z - g) % fine], v)
                zw = fine * zc + z
                put(h, z, jnp.where((zw >= W) & (zw < W + lanes), v, 0.0))

    for f in range(FIELDS):
        def put(h, z, v, f=f):
            sxs[0, f, h, z] = v[0:W]
            sxs[1, f, h, z] = v[W:2 * W]
        spread(lambda y, f=f: strip[f, y], put, 2 * W)
    pl.semaphore_wait(barrier, count)
    start(static_strips(still, 8))
    start(static_copies(False))
    start(static_copies(True))
    start(static_strips(moving, 10))

    def cells(f):
        return cc.at[0] if f == CONC else stat.at[f]

    for f, ref in ((CONC, c_in), (TEMP, t_in), (PERM, o_pm), (LIQ, o_liq)):
        for r in range(0, n, 16):
            def put(h, z, v, f=f, r=r):
                cells(f)[h, z, mid + r:mid + r + 16, :] = v
            spread(lambda y, ref=ref, r=r: ref[y, r:r + 16], put, 16)

    def own_sum(values, rows):
        zc = lane(rows) % per
        out = jnp.zeros((rows, lanes), f32)
        for first in sorted({0, W % fine, (W + lanes) % fine}):
            last = min([e for e in (W % fine, (W + lanes) % fine, fine) if e > first])
            part = values[first]
            for z in range(first + 1, last):
                part = part + values[z]
            zw = fine * zc + first
            out = out + jnp.where((zw >= W) & (zw < W + lanes), part, 0.0)
        return out

    def send_totals(s, along_x):
        parts = [(0, 8), (n - 8, 8)] if along_x else [(0, n)]
        sums = []
        for h in range(HALVES):
            for row, rows in parts:
                conc = own_sum([cc[s, h, z, pl.ds(mid + row, rows), :] for z in range(fine)], rows)
                sums.append(split(tt0[h, row:row + rows] + 0.2 * conc))
        tot = jnp.dot(jnp.concatenate(sums, axis=0), wts[2 * lanes:4 * lanes], preferred_element_type=f32)
        slot = lane(8) % per
        out = jnp.zeros((8, lanes), f32)
        places = [h * blocks + j for h in range(HALVES) for row, rows in parts for j in range(row // 8, (row + rows) // 8)]
        for i, place in enumerate(places):
            out = jnp.where(slot == place, tot[8 * i:8 * i + 8], out)
        (td if along_x else ts)[s] = out
        start(total_copies(s, along_x))

    def edge(h, rows):
        return lane(rows) < per if h == 0 else lane(rows) >= lanes - per

    shift = (per, lanes - per)

    def turn(s):
        for h in range(HALVES):
            for z in range(fine):
                cr[h, z] = jnp.where(edge(h, n), 0.0, pltpu.roll(cc[s, 1 - h, z, center, :], shift[h], 1))

    for h in range(HALVES):
        tt0[h] = own_sum([1.0 - 0.3 * stat[TEMP, h, z, center, :] for z in range(fine)], n)
    send_totals(0, True)
    send_totals(0, False)
    turn(0)

    def insert(dst, packed, row, rows):
        zc, at_rows = lane(rows) % per, pl.ds(LO + row, rows)
        for h in range(HALVES):
            for k in range(2 * W):
                at, z = divmod(k if k < W else lanes + k, fine)
                moved = pltpu.roll(packed, (at - h * 2 * W - k) % lanes, 1)
                dst[h, z, at_rows, :] = jnp.where(zc == at, moved, dst[h, z, at_rows, :])

    def insert_strips(dst, strips, corners):
        for h in range(HALVES):
            for z in range(fine):
                dst[h, z, top, :] = strips(0, h, z)
                dst[h, z, bottom, :] = strips(1, h, z)
        for b in range(2):
            hz[b] = jnp.where(k_e < W, corners(b, 0), corners(b, 1))
            insert(dst, hz[b], b * (n + W), W)

    k_n, k_e = lane(n) % (2 * W), lane(W) % (2 * W)

    def coefficients(row, rows):
        here, up, down, flat = pl.ds(LO + row, rows), pl.ds(LO + row + 1, rows), pl.ds(LO + row - 1, rows), pl.ds(row, rows)
        beside = [edge(h, rows) for h in range(HALVES)]
        for h in range(HALVES):
            for z in range(fine):
                pm = stat[PERM, h, z, here, :]
                over = stat[PERM, h, z + 1, here, :] if z < fine - 1 else pltpu.roll(stat[PERM, h, 0, here, :], lanes - 1, 1)
                under = stat[PERM, h, z - 1, here, :] if z > 0 else pltpu.roll(stat[PERM, h, fine - 1, here, :], 1, 1)
                cross = jnp.where(beside[h], 0.0, pltpu.roll(stat[PERM, 1 - h, z, here, :], shift[h], 1))
                c = [0.5 * (pm + other) for other in (
                    stat[PERM, h, z, up, :], stat[PERM, h, z, down, :], stat[PERM, 1 - h, z, here, :], cross, over, under)]
                total = c[0] + c[1] + c[2] + c[3] + c[4] + c[5]
                real = pm > 0.0
                inv = jnp.where(real, 1.0 / jnp.where(real, total, 1.0), 0.0)
                cxp[h, z, here, :] = c[0]
                if h == 0:
                    cys[z, here, :] = c[2]
                cyr[h, z, here, :] = c[3]
                cz[h, z + 1, here, :] = c[4]
                if z == 0:
                    cz[h, 0, here, :] = c[5]
                axp[h, z, flat] = c[0] * inv
                axm[h, z, flat] = c[1] * inv
                ays[h, z, flat] = c[2] * inv
                ayr[h, z, flat] = jnp.where(beside[h], 0.0, c[3] * inv)
                azp[h, z, flat] = c[4] * inv
                azm[h, z, flat] = c[5] * inv
                liq, t = stat[LIQ, h, z, here, :], stat[TEMP, h, z, here, :]
                srcn[h, z, flat] = 2.0 * liq * (1.0 - liq) * t * inv
                tt[h, z, flat] = jnp.where(real, 1.0 - 0.3 * t, 0.0)
                gr[h, z, flat] = jnp.where(real, gravity, 0.0)

    def keep(sweep, h, z, row, rows, v):
        p, r = press[sweep], turned[sweep]
        at_rows = pl.ds(LO + row, rows)
        p[h, z + 1, at_rows, :] = v
        r[1 - h, z, pl.ds(row, rows), :] = pltpu.roll(v, shift[1 - h], 1)
        if z == 0:
            p[h, fine + 1, at_rows, :] = pltpu.roll(v, lanes - 1, 1)
        if z == fine - 1:
            p[h, 0, at_rows, :] = pltpu.roll(v, 1, 1)

    order = [0, fine - 1] + list(range(1, fine - 1))

    def carried(flow, own, other):
        return flow * jnp.where(flow > 0.0, own, other)

    def forces(s, row, rows):
        here, flat = pl.ds(LO + row, rows), pl.ds(row, rows)
        first_lane = lane(rows) % per == 0
        for h in range(HALVES):
            for z in range(fine):
                rh[h, z, flat, :] = tt[h, z, flat, :] + 0.2 * cc[s, h, z, here, :]
            before = rh[h, 0, flat, :]
            for z in range(1, W):
                before = before + rh[h, z, flat, :]
            run = jnp.where(first_lane, -before, 0.0)
            lo = half * (pltpu.roll(rh[h, fine - 1, flat, :], 1, 1) + rh[h, 0, flat, :])
            lift[h, 0, here, :] = lo
            for z in range(fine):
                rho = rh[h, z, flat, :]
                press[0][h, z + 1, here, :] = run + 0.5 * rho
                run = run + rho
                other = rh[h, z + 1, flat, :] if z < fine - 1 else pltpu.roll(rh[h, 0, flat, :], lanes - 1, 1)
                hi = half * (rho + other)
                lift[h, z + 1, here, :] = hi
                bb[h, z, flat, :] = srcn[h, z, flat, :] - azp[h, z, flat, :] * hi + azm[h, z, flat, :] * lo
                lo = hi
            sm[h, flat, :] = run

    def above(parts):
        rows_in = [(h, pl.ds(row, rows)) for h in range(HALVES) for row, rows in parts]
        both = jnp.concatenate([jnp.concatenate([split(sm[h, at, :]), split(off[h, at, :])], axis=1) for h, at in rows_in], axis=0)
        base = jnp.dot(both, wts[...], preferred_element_type=f32)
        done = 0
        for h in range(HALVES):
            for row, rows in parts:
                ab[h, pl.ds(row, rows), :] = base[done:done + rows]
                done += rows

    def heads(row, rows):
        here, flat = pl.ds(LO + row, rows), pl.ds(row, rows)
        for z in order:
            for h in range(HALVES):
                keep(0, h, z, row, rows, gr[h, z, flat, :] * (press[0][h, z + 1, here, :] + ab[h, flat, :]))

    def relax(sweep, row, rows):
        old, rold = press[sweep], turned[sweep]
        here, flat = pl.ds(LO + row, rows), pl.ds(row, rows)
        up, down = pl.ds(LO + row + 1, rows), pl.ds(LO + row - 1, rows)
        for z in order:
            for h in range(HALVES):
                v = bb[h, z, flat, :] + axp[h, z, flat, :] * old[h, z + 1, up, :] + axm[h, z, flat, :] * old[h, z + 1, down, :]
                v = v + (ays[h, z, flat, :] * old[1 - h, z + 1, here, :] + ayr[h, z, flat, :] * rold[h, z, flat, :])
                v = v + (azp[h, z, flat, :] * old[h, z + 2, here, :] + azm[h, z, flat, :] * old[h, z, here, :])
                keep(sweep + 1, h, z, row, rows, v)

    def ends(row):
        return [(row, 8), (wide - 8 - row, 8)]

    def received(s, side):
        total = tr[s, side, 0]
        for d in range(1, nz - 1):
            total = total + tr[s, side, d]
        return total

    old, rold = press[SWEEPS], turned[SWEEPS]

    def step(s, final):
        lead = W if s > 0 else 8
        def transport(row, rows):
            here, up, down = pl.ds(mid + row, rows), pl.ds(mid + row + 1, rows), pl.ds(mid + row - 1, rows)
            flat, inner = pl.ds(row, rows), pl.ds(W + row, rows)
            slab = jnp.zeros((rows, lanes), f32)
            k_slab = lane(rows) % per
            wrap = [(pltpu.roll(cc[s, h, fine - 1, here, :], 1, 1), pltpu.roll(cc[s, h, 0, here, :], lanes - 1, 1))
                    for h in range(HALVES)]
            low = [carried(cz[h, 0, here, :] * (old[h, 0, here, :] - old[h, 1, here, :] + lift[h, 0, here, :]),
                           wrap[h][0], cc[s, h, 0, here, :]) for h in range(HALVES)]
            for z in range(fine):
                ps = [old[h, z + 1, here, :] for h in range(HALVES)]
                cs = [cc[s, h, z, here, :] for h in range(HALVES)]
                between = carried(cys[z, here, :] * (ps[0] - ps[1]), cs[0], cs[1])
                for h in range(HALVES):
                    p, c = ps[h], cs[h]
                    change = carried(cxp[h, z, here, :] * (p - old[h, z + 1, up, :]), c, cc[s, h, z, up, :])
                    change = change + carried(cxp[h, z, down, :] * (p - old[h, z + 1, down, :]), c, cc[s, h, z, down, :])
                    side = jnp.where(edge(h, rows), 0.0, rold[h, z, inner, :])
                    change = change + carried(cyr[h, z, here, :] * (p - side), c, cr[h, z, flat, :])
                    change = change + between if h == 0 else change - between
                    over = cc[s, h, z + 1, here, :] if z < fine - 1 else wrap[h][1]
                    high = carried(cz[h, z + 1, here, :] * (p - old[h, z + 2, here, :] + lift[h, z + 1, here, :]), c, over)
                    change = change + (high - low[h])
                    low[h] = high
                    fresh = c - rl[h, z, flat, :] * change
                    cc[s + 1, h, z, here, :] = fresh
                    if final:
                        continue
                    if row == 0:
                        xs[s + 1, 0, h, z] = fresh[0:W]
                    if row + rows == n:
                        xs[s + 1, 1, h, z] = fresh[rows - W:rows]
                    for j in range(2 * W):
                        at, zj = divmod(lanes + j if j < W else j, fine)
                        if zj == z:
                            k = h * 2 * W + j
                            slab = jnp.where(k_slab == k, pltpu.roll(fresh, (k - at) % lanes, 1), slab)
            if final:
                return
            zs[s + 1, flat, :] = slab
            if row == 0:
                es[s + 1, 0] = slab[0:W]
            if row + rows == n:
                es[s + 1, 1] = slab[rows - W:rows]

        slot = lane(8) % per
        if s > 0:
            arrive(halo_copies(s, False))
            insert(cc.at[s], jnp.where(k_n < W, zr[s, 0], zr[s, 1]), W, n)
        else:
            arrive(static_copies(True))
            for f in range(FIELDS):
                insert(cells(f), jnp.where(k_n < W, szr[0, f], szr[1, f]), W, n)
            zc_n = lane(n) % per
            for h in range(HALVES):
                for z in range(fine):
                    zw = fine * zc_n + z
                    rl[h, z] = jnp.where((zw >= W) & (zw < W + lanes),
                                         SOLUTE_RATE / (stat[LIQ, h, z, center, :] + 0.1), 0.0)
            coefficients(lead, wide - 2 * lead)
        inner = (lead, wide - 2 * lead)
        forces(s, *inner)
        arrive(total_copies(s, False))
        below = received(s, 1)
        for h in range(HALVES):
            for j in range(blocks):
                off[h, W + 8 * j:W + 8 * j + 8] = jnp.where(slot == h * blocks + j, below, 0.0)
        above([inner])
        heads(*inner)
        for sweep in range(SWEEPS):
            relax(sweep, lead + 1 + sweep, wide - 2 * (lead + 1 + sweep))
        transport(lead, n - 2 * lead)

        def outs(part, row, rows):
            at, to = pl.ds(mid + row, rows), pl.ds(row, rows)
            return [pltpu.make_async_copy(old.at[:, pl.ds(1, fine), at, :], p_out.at[:, :, to, :], out_sem.at[2 * part]),
                    pltpu.make_async_copy(cc.at[s + 1, :, :, at, :], c_out.at[:, :, to, :], out_sem.at[2 * part + 1])]

        if final:
            leaving = outs(0, 8, n - 16)
            for out in leaving:
                out.start()

        if s > 0:
            arrive(halo_copies(s, True))
            insert_strips(cc.at[s], lambda b, h, z: xr[s, b, h, z], lambda b, side: er[s, b, side])
        else:
            arrive(static_strips(still, 8))
            arrive(static_copies(False))

            def place(f):
                insert_strips(cells(f), lambda b, h, z: sxr[b, f, h, z], lambda b, side: ser[b, side, f])

            for f in (PERM, TEMP, LIQ):
                place(f)
            for end in ends(0):
                coefficients(*end)
            arrive(static_strips(moving, 10))
            place(CONC)
        for end in ends(0):
            forces(s, *end)
        arrive(total_copies(s, True))
        left, right = received(s, 0), received(s, 2)
        for h in range(HALVES):
            off[h, 0:W] = jnp.where(slot == h * blocks + blocks - 1, left, 0.0)[8 - W:8]
            off[h, W + n:wide] = jnp.where(slot == h * blocks, right, 0.0)[0:W]
        above(ends(0))
        for end in ends(0):
            heads(*end)
        for sweep in range(SWEEPS):
            for end in ends(sweep + 1):
                relax(sweep, *end)
        if s > 0:
            sent(halo_copies(s, True))
            sent(halo_copies(s, False))
        else:
            sent(static_strips(still, 8))
            sent(static_strips(moving, 10))
            sent(static_copies(True))
            sent(static_copies(False))
        sent(total_copies(s, True))
        sent(total_copies(s, False))
        if not final:
            transport(0, 8)
            transport(n - 8, 8)
            send_totals(s + 1, False)
            start(halo_copies(s + 1, False))
            start(halo_copies(s + 1, True))
            send_totals(s + 1, True)
            turn(s + 1)
        else:
            transport(0, 8)
            transport(n - 8, 8)
            rest = outs(1, 0, 8) + outs(2, n - 8, 8)
            for out in rest:
                out.start()
            for out in leaving + rest:
                out.wait()

    for s in range(STEPS):
        step(s, s == STEPS - 1)


def hand_out(p, c, p_out, c_out, p_cells, c_cells, p_block, c_block, in_sem, out_sem):
    fine, n, lanes = p.shape[1:]
    per = lanes // GROUPS
    parts = [pl.ds(r, PART) for r in range(0, n, PART)]
    fields = ((p, p_cells, p_block, p_out), (c, c_cells, c_block, c_out))
    loads = [[pltpu.make_async_copy(src.at[:, :, part, :], cells.at[:, :, part, :], in_sem.at[a, i])
              for a, (src, cells, _, _) in enumerate(fields)] for i, part in enumerate(parts)]
    stores = [[pltpu.make_async_copy(block.at[:, part, :], dst.at[:, part, :], out_sem.at[a, i])
               for a, (_, _, block, dst) in enumerate(fields)] for i, part in enumerate(parts)]
    for pair in loads:
        for load in pair:
            load.start()
    ln = lax.broadcasted_iota(jnp.int32, (PART, lanes), 1)
    res, grp = (ln + W) % fine, ln // per
    for i, part in enumerate(parts):
        for a, (_, cells, block, _) in enumerate(fields):
            loads[i][a].wait()
            for h in range(HALVES):
                vals = [cells[h, z, part, :] for z in range(fine)]
                moved = []
                for d in range(fine):
                    comb = vals[d]
                    for g in range(1, GROUPS):
                        comb = jnp.where(grp == g, vals[(g + d) % fine], comb)
                    g = jnp.minimum((res - d + fine) % fine, GROUPS - 1)
                    moved.append(jnp.take_along_axis(comb, g * per + (ln + W) // fine, axis=1, mode="promise_in_bounds"))
                for g in range(GROUPS):
                    v = moved[0]
                    for d in range(1, fine):
                        v = jnp.where(res == (g + d) % fine, moved[d], v)
                    block[HALVES * g + h, part, :] = v
            stores[i][a].start()
    for pair in stores:
        for store in pair:
            store.wait()


def on_device(nx, nz, *args):
    ny, n, lanes = args[0].shape
    wide = n + 2 * W
    rows = wide + 2 * LO
    per = lanes // GROUPS
    fine = -(-(lanes + 2 * W) // per)
    copies = 8 + 3 * (nz - 1)

    def vmem(*shape):
        return pltpu.VMEM(shape, jnp.float32)

    padded, plain, own = (HALVES, fine, rows, lanes), (HALVES, fine, wide, lanes), (HALVES, fine, n, lanes)
    slots = (HALVES, fine + 2, rows, lanes)
    scratch = [pltpu.VMEM((ny, n, lanes), a.dtype) for a in args]
    scratch += [vmem(ny, n, lanes)] * 2 + [vmem(FIELDS, ny, 2 * W, lanes)]
    scratch += [vmem(FIELDS - 1, *padded), vmem(STEPS + 1, *padded), vmem(*own)]
    scratch += [vmem(*slots)] * W + [vmem(*plain)] * W
    scratch += [vmem(*plain)] * 10
    scratch += [vmem(*padded), vmem(fine, rows, lanes), vmem(*padded), vmem(HALVES, fine + 1, rows, lanes),
                vmem(HALVES, fine + 1, rows, lanes), vmem(*own), vmem(*plain)]
    scratch += [pltpu.VMEM((4 * lanes, lanes), jnp.bfloat16), vmem(2, W, lanes)] + [vmem(HALVES, wide, lanes)] * 3
    scratch += [vmem(HALVES, n, lanes)]
    scratch += [vmem(STEPS, 2, HALVES, fine, W, lanes)] * 2
    scratch += [vmem(STEPS, n, lanes), vmem(STEPS, 2, n, lanes)]
    scratch += [vmem(STEPS, 2, W, lanes), vmem(STEPS, 2, 2, W, lanes)]
    scratch += [vmem(STEPS, 8, lanes)] * 2 + [vmem(STEPS, 3, nz - 1, 8, lanes)]
    scratch += [vmem(2, FIELDS, HALVES, fine, W, lanes)] * 2
    scratch += [vmem(FIELDS, n, lanes), vmem(2, FIELDS, n, lanes), vmem(2, FIELDS, W, lanes), vmem(2, 2, FIELDS, W, lanes)]
    scratch += [pltpu.SemaphoreType.DMA((copies,)), pltpu.SemaphoreType.DMA((STEPS, copies))] + [pltpu.SemaphoreType.DMA((12,))] * 2
    scratch += [pltpu.SemaphoreType.DMA((5,)), pltpu.SemaphoreType.DMA((6,))]
    cells = pl.pallas_call(
        functools.partial(kernel, nx, nz),
        out_shape=[jax.ShapeDtypeStruct(own, jnp.float32)] * 2,
        in_specs=[pl.BlockSpec(memory_space=pltpu.HBM)] * 5,
        out_specs=[pl.BlockSpec(memory_space=pltpu.HBM)] * 2,
        scratch_shapes=scratch,
        compiler_params=pltpu.CompilerParams(
            collective_id=0, has_side_effects=True, vmem_limit_bytes=63 * 1024 * 1024),
    )(*args)
    return tuple(pl.pallas_call(
        hand_out,
        out_shape=[jax.ShapeDtypeStruct((ny, n, lanes), jnp.float32)] * 2,
        in_specs=[pl.BlockSpec(memory_space=pltpu.HBM)] * 2,
        out_specs=[pl.BlockSpec(memory_space=pltpu.HBM)] * 2,
        scratch_shapes=[vmem(*own)] * 2 + [vmem(ny, n, lanes)] * 2 + [pltpu.SemaphoreType.DMA((2, n // PART))] * 2,
        compiler_params=pltpu.CompilerParams(vmem_limit_bytes=63 * 1024 * 1024),
    )(*cells))


def solution(mesh):
    placed = P(None, "gx", "gz")
    return jax.shard_map(
        functools.partial(on_device, mesh.shape["gx"], mesh.shape["gz"]),
        mesh=mesh,
        in_specs=(placed,) * 5,
        out_specs=(placed, placed),
        check_vma=False,
    )
```
